128 devices in a mesh: ind: 32 (over x, y, z_hi), snp: 4 (over z_lo, core).
Axes of the slice: x: 4, y: 4, z: 4 (z_hi: 2, z_lo: 2; z = z_hi * 2 + z_lo), core: 2. Of those that a mesh axis runs over, the one named last changes fastest.
Arguments:
- genotypes: bfloat16 [2, 32768, 16384], P(None, 'ind', 'snp'), may hold values from 0 to 2, as said below
- snp_index: int32 [2, 16384], P(None, 'snp'), may hold values from 0 to 16383, as said below
- props: float32 [16, 32768], P(None, 'ind'), as said below
- freq_table: float32 [16, 65536], P(None, 'snp'), may hold values from 0.05 to 0.95
Outputs:
- log_props: float32 [16, 32768], P(None, 'ind')
- freq_out: float32 [16, 65536], P(None, 'snp')
The draws below stay inside these ranges and needn't reach their ends.
Inputs may be any that keep to these rules, and one draw needn't show every extreme that they name: `snp_index`: within one step and one block of 4096 columns the entries are distinct; every such block holds 0 and 16383. `props`: each column is positive and sums to one. `genotypes`: whole numbers 0, 1, 2.
All inputs are finite; a program needn't handle non-finite values.
Results may differ from the reference program's by a relative error of at most 0.0003.
Values sent between devices are 32-bit elements; how exact they have to be, the bound alone decides.
No kernel may reach another device: no remote copies, remote signals or barrier semaphores. Data moves between devices by JAX's collectives and lax.ppermute only.
A program may use at most 192 MiB of HBM per device.

```python
import jax
import jax.numpy as jnp
from jax import lax

K = 16
IND_DEV = 1024
MB_DEV = 4096
STEPS = 2
TAB_DEV = 16384
IND = 32768
MB = 16384
TAB = 65536


def draw_genotypes(key, part):
    key = jax.random.fold_in(key, 3)
    values = jax.random.randint(key, (STEPS, IND, MB), 0, 3)
    return values.astype(jnp.float32).astype(jnp.bfloat16)


def draw_props(key, part):
    key = jax.random.fold_in(key, 5)
    level = jax.random.uniform(key, (K, IND), jnp.float32)
    weights = jnp.exp(jnp.log(0.05) + level * jnp.log(20.0))
    return weights / jnp.sum(weights, axis=0, keepdims=True)


def draw_snp_index(key, part):
    key = jax.random.fold_in(key, 7)
    count = STEPS * (MB // MB_DEV)
    keys = jax.random.split(key, count)

    def one_block(block_key):
        first_key, second_key = jax.random.split(block_key)
        inner = jax.random.permutation(first_key, TAB_DEV - 2)[:MB_DEV - 2] + 1
        ends = jnp.array([0, TAB_DEV - 1], jnp.int32)
        whole = jnp.concatenate([inner.astype(jnp.int32), ends])
        return jax.random.permutation(second_key, whole)
    rows = jax.vmap(one_block)(keys)
    return rows.reshape(STEPS, MB).astype(jnp.int32)


def block_scale(rng, extent, cuts, low, top_value):
    def one(dim, parts):
        heights = jax.random.uniform(jax.random.fold_in(jax.random.fold_in(rng, 6), dim), (parts,), jnp.float32, low / len(cuts), top_value / len(cuts))
        return jnp.repeat(jnp.exp(heights), extent[dim] // parts).reshape((-1,) + (1,) * (len(extent) - dim - 1))

    loudness = one(*cuts[0])
    for cut in cuts[1:]:
        loudness = loudness * one(*cut)
    return loudness


def setup_inputs(seed: int = 0) -> dict:
    key_of = jax.random.split(jax.random.key(seed), 5)
    return {
        "genotypes": draw_genotypes(jax.random.fold_in(key_of[4], 71), 0),
        "snp_index": draw_snp_index(jax.random.fold_in(key_of[4], 71), 0),
        "props": draw_props(jax.random.fold_in(key_of[4], 71), 0),
        "freq_table": jnp.clip(0.05 + 0.9 * jax.random.uniform(key_of[3], (K, TAB), jnp.float32) ** block_scale(key_of[3], (K, TAB), ((1, 4),), -0.2, 0.2), 0.05, 0.95),
    }


def reference(genotypes, snp_index, props, freq_table):
    highest = lax.Precision.HIGHEST
    nblock = IND // IND_DEV
    for step in range(STEPS):
        offsets = ((jnp.arange(MB) // MB_DEV) * TAB_DEV).astype(jnp.int32)
        cols = (snp_index[step].astype(jnp.int32) + offsets).astype(jnp.int32)
        freq = jnp.take(freq_table, cols, axis=1)
        geno_blocks = genotypes[step].reshape(nblock, IND_DEV, MB)
        prop_blocks = props.reshape(K, nblock, IND_DEV).transpose(1, 0, 2)

        def one(carry, item):
            geno, local = item
            geno = geno.astype(jnp.float32)
            hmix = jnp.einsum("ki,kj->ij", local, freq, precision=highest)
            ratio_a = geno / hmix
            ratio_b = (2.0 - geno) / (1.0 - hmix)
            prop_num = jnp.einsum("kj,ij->ki", freq, ratio_a, precision=highest) + jnp.einsum("kj,ij->ki", 1.0 - freq, ratio_b, precision=highest)
            sum_a = jnp.einsum("ki,ij->kj", local, ratio_a, precision=highest)
            sum_b = jnp.einsum("ki,ij->kj", local, ratio_b, precision=highest)
            return carry + jnp.stack([sum_a, sum_b]), prop_num

        start = jnp.zeros((2, K, MB), jnp.float32)
        sums, prop_nums = lax.scan(one, start, (geno_blocks, prop_blocks))
        acc_a = freq * sums[0]
        acc_b = (1.0 - freq) * sums[1]
        new_freq = acc_a / (acc_a + acc_b)
        prop_num = prop_nums.transpose(1, 0, 2).reshape(K, IND)
        props = props * prop_num / (2.0 * MB)
        freq_table = freq_table.at[:, cols].set(new_freq)
    return jnp.log(props), freq_table
```

```python
import functools

import jax
import jax.numpy as jnp
import numpy as np
from jax import lax
from jax.experimental import pallas as pl
from jax.experimental.pallas import tpu as pltpu
from jax.sharding import PartitionSpec as P

STEPS = 2
K = 16
BLOCK = 1024
NT = (((1,), (1,)), ((), ()))

SCALE_I = ((np.arange(64) * 37 + 5) % 128 + 128).astype(np.float32) / 256
SCALE_J = ((np.arange(128) * 53 + 11) % 128 + 128).astype(np.float32) / 256


def split3(x):
    one = x.astype(jnp.bfloat16)
    rest = x - one.astype(jnp.float32)
    two = rest.astype(jnp.bfloat16)
    three = (rest - two.astype(jnp.float32)).astype(jnp.bfloat16)
    return one, two, three


def em_kernel(scale_ref, w_ref, geno_ref, props_ref, freq_ref, sums_ref, num_ref, pt_ref, ps_ref):
    j = pl.program_id(0)
    n_ind = geno_ref.shape[1]
    n_snp = geno_ref.shape[2]

    @pl.when(j == 0)
    def _():
        scaled = props_ref[...] * scale_ref[0:1, :n_ind]
        p1, p2, p3 = split3(scaled)
        ps_ref[...] = jnp.concatenate([p1, p2], 0)
        f = lambda v: v.astype(jnp.float32)
        stacked = jnp.concatenate([f(p1), f(p1), f(p2), f(p1), f(p2), f(p3)], 0)
        pt_ref[...] = stacked.T.astype(jnp.bfloat16)

    freq = freq_ref[...]
    scale_j = scale_ref[1:2, :n_snp]
    f1, f2, f3 = split3(freq * scale_j)
    b1, b2, _ = split3((1.0 - freq) * scale_j)
    h = jnp.dot(pt_ref[...], jnp.concatenate([f1, f2, f1, f3, f2, f1], 0), preferred_element_type=jnp.float32)
    w = jnp.concatenate([w_ref[...]] * (n_snp // 128), 1)
    w = jnp.concatenate([w] * (n_ind // 64), 0)
    inv_a = pl.reciprocal(h, approx=True).astype(jnp.bfloat16)
    inv_b = pl.reciprocal(w - h, approx=True).astype(jnp.bfloat16)
    geno = geno_ref[0]
    ratio_a = geno * inv_a
    ratio_b = (jnp.bfloat16(2) - geno) * inv_b
    ps = ps_ref[...]
    sum_a = jnp.dot(ps, ratio_a, preferred_element_type=jnp.float32)
    sum_b = jnp.dot(ps, ratio_b, preferred_element_type=jnp.float32)
    sums_ref[0, 0:K, :] = sum_a[:K] + sum_a[K:]
    sums_ref[0, K:, :] = sum_b[:K] + sum_b[K:]
    num = lax.dot_general(jnp.concatenate([f1, f2], 0), ratio_a, NT, preferred_element_type=jnp.float32)
    num += lax.dot_general(jnp.concatenate([b1, b2], 0), ratio_b, NT, preferred_element_type=jnp.float32)
    num = num[:K] + num[K:]

    @pl.when(j == 0)
    def _():
        num_ref[...] = num

    @pl.when(j != 0)
    def _():
        num_ref[...] += num


def em_sums(step, genotypes, props, freq):
    n_ind, n_snp = genotypes.shape[1:]
    width = max(n_ind, BLOCK)
    scale = np.stack([np.tile(SCALE_I, width // 64), np.tile(SCALE_J, width // 128)])
    w = SCALE_I[:, None] * SCALE_J[None, :]
    fixed = lambda j: (0, 0)
    return pl.pallas_call(
        em_kernel,
        grid=(n_snp // BLOCK,),
        in_specs=[
            pl.BlockSpec((2, width), fixed),
            pl.BlockSpec((64, 128), fixed),
            pl.BlockSpec((1, n_ind, BLOCK), lambda j: (step, 0, j)),
            pl.BlockSpec((K, n_ind), fixed),
            pl.BlockSpec((K, BLOCK), lambda j: (0, j)),
        ],
        out_specs=[
            pl.BlockSpec((1, 2 * K, BLOCK), lambda j: (j, 0, 0)),
            pl.BlockSpec((K, n_ind), fixed),
        ],
        out_shape=[
            jax.ShapeDtypeStruct((n_snp // BLOCK, 2 * K, BLOCK), jnp.float32),
            jax.ShapeDtypeStruct((K, n_ind), jnp.float32),
        ],
        scratch_shapes=[pltpu.VMEM((n_ind, 6 * K), jnp.bfloat16), pltpu.VMEM((2 * K, n_ind), jnp.bfloat16)],
        compiler_params=pltpu.CompilerParams(vmem_limit_bytes=48 << 20),
        cost_estimate=pl.CostEstimate(flops=10 * K * n_ind * n_snp, bytes_accessed=2 * n_ind * n_snp, transcendentals=0),
        name="em_sums",
    )(jnp.asarray(scale), jnp.asarray(w), genotypes, props, freq)


def swap(value, axis, bits):
    size = lax.axis_size(axis)
    return lax.ppermute(value, axis, [(i, i ^ bits) for i in range(size)])


def all_sum4(value, axis, unit):
    one, two, three = (swap(value, axis, d * unit) for d in (1, 2, 3))
    return (value + one) + (two + three)


def per_device(genotypes, snp_index, props, freq_table):
    batch_total = genotypes.shape[2] * lax.axis_size("snp")
    n_ind = genotypes.shape[1]
    spot = lax.axis_index("ind") // 8
    scale_i = jnp.asarray(np.tile(SCALE_I, n_ind // 64))
    for step in range(STEPS):
        rows = snp_index[step]
        freq = jnp.take(freq_table, rows, axis=1)
        sums, num = em_sums(step, genotypes, props, freq)
        block = lambda d: lax.dynamic_index_in_dim(sums, spot ^ d, 0, False)
        parts = [swap(block(d), "ind", 8 * d) for d in (1, 2, 3)]
        mine = (block(0) + parts[0]) + (parts[1] + parts[2])
        mine = all_sum4(mine, "ind", 2)
        mine = mine + swap(mine, "ind", 1)
        old = lax.dynamic_slice_in_dim(freq, spot * BLOCK, BLOCK, 1)
        acc_a = old * mine[:K]
        acc_b = (1.0 - old) * mine[K:]
        new = acc_a / (acc_a + acc_b)
        new_freq = jnp.zeros_like(freq)
        for d in range(4):
            piece = new if d == 0 else swap(new, "ind", 8 * d)
            new_freq = lax.dynamic_update_slice_in_dim(new_freq, piece, (spot ^ d) * BLOCK, 1)
        prop_num = all_sum4(num, "snp", 1)
        props = props * (prop_num * scale_i) / (2.0 * batch_total)
        freq_table = freq_table.at[:, rows].set(new_freq)
    return (jnp.log(props), freq_table)


def solution(mesh):
    placed = (P(None, "ind", "snp"), P(None, "snp"), P(None, "ind"), P(None, "snp"))
    return jax.shard_map(
        per_device,
        mesh=mesh,
        in_specs=placed,
        out_specs=(P(None, "ind"), P(None, "snp")),
        check_vma=False,
    )
```

```python
import functools

import jax
import jax.numpy as jnp
import numpy as np
from jax import lax
from jax.experimental import pallas as pl
from jax.experimental.pallas import tpu as pltpu
from jax.sharding import PartitionSpec as P

STEPS = 2
K = 16
LANES = 128
BLOCK = 1024
TILES = BLOCK // LANES
NN = (((1,), (0,)), ((), ()))
NT = (((1,), (1,)), ((), ()))
TN = (((0,), (0,)), ((), ()))
MIB = 1 << 20

def scale_of_ind(i):
    return ((i % 64 * 37 + 5) % 128 + 128).astype(jnp.float32) * (1.0 / 256)


def scale_of_snp(j):
    return ((j % 128 * 53 + 11) % 128 + 128).astype(jnp.float32) * (1.0 / 256)


def iota(shape, dim):
    return lax.broadcasted_iota(jnp.int32, shape, dim)


def estimate(us):
    return pl.CostEstimate(flops=0, bytes_accessed=int(us * 3.5e6), transcendentals=0)


def split3(x):
    one = x.astype(jnp.bfloat16)
    rest = x - one.astype(jnp.float32)
    two = rest.astype(jnp.bfloat16)
    three = (rest - two.astype(jnp.float32)).astype(jnp.bfloat16)
    return one, two, three


def dot_exact(left, right, dims):
    return lax.dot_general(
        left.astype(jnp.bfloat16), right.astype(jnp.bfloat16), dims, preferred_element_type=jnp.float32
    )


def one_hot(count, value):
    ids = lax.broadcasted_iota(jnp.int32, (count, value.shape[1]), 0)
    return (ids == value).astype(jnp.float32).astype(jnp.bfloat16)


def halves(x):
    hi = jnp.floor(x * (1.0 / LANES))
    return hi, x - LANES * hi


def look_up(table, hot_hi, hot_lo):
    hi, lo = halves(table)
    pick = hot_lo.astype(jnp.float32)
    first = jnp.sum(pick * dot_exact(hi, hot_hi, TN), 0, keepdims=True)
    return LANES * first + jnp.sum(pick * dot_exact(lo, hot_hi, TN), 0, keepdims=True)


def index_kernel(step, rows_ref, pos_ref, perm_ref, start_ref, match_ref):
    n_blocks = rows_ref.shape[1] // BLOCK
    row = lax.broadcasted_iota(jnp.int32, (LANES, LANES), 0)
    col = lax.broadcasted_iota(jnp.int32, (LANES, LANES), 1)
    below = (col < row).astype(jnp.float32)
    above = (row < col).astype(jnp.float32)
    ones = jnp.ones((LANES, LANES), jnp.float32)
    local = lax.broadcasted_iota(jnp.int32, (1, BLOCK), 1).astype(jnp.float32)
    local_hi, local_lo = (v.astype(jnp.bfloat16) for v in halves(local))
    pos = jnp.full((LANES, LANES), -1.0, jnp.float32)
    for b in range(n_blocks):
        rows = rows_ref[step : step + 1, b * BLOCK : (b + 1) * BLOCK]
        hot_hi, hot_lo = one_hot(LANES, rows >> 7), one_hot(LANES, rows & 127)
        mask = dot_exact(hot_hi, hot_lo, NT)
        rank = dot_exact(dot_exact(below, mask, NN), ones, NN) + dot_exact(mask, above, NN)
        counts = dot_exact(jnp.ones((16, BLOCK), jnp.float32), hot_hi, NT)
        before = dot_exact(counts, above, NN)[:8].astype(jnp.int32)
        start_ref[b] = jnp.minimum(before >> 7, TILES - 2)
        pos = jnp.where(mask > 0.5, rank + float(b * BLOCK), pos)
        rank_j = look_up(rank, hot_hi, hot_lo).astype(jnp.int32)
        hot_rank = one_hot(16, rank_j >> 7)
        hot_low = one_hot(LANES, rank_j & 127)
        perm = LANES * dot_exact(hot_rank * local_hi, hot_low, NT) + dot_exact(hot_rank * local_lo, hot_low, NT)
        perm_ref[b] = perm[:TILES].astype(jnp.int32)
    pos_ref[...] = pos.astype(jnp.int32)
    for b in range(n_blocks if step == 0 else 0):
        span = slice(b * BLOCK, (b + 1) * BLOCK)
        rows = rows_ref[1:2, span]
        found = look_up(pos + 1.0, one_hot(LANES, rows >> 7), one_hot(LANES, rows & 127))
        match_ref[0:1, span] = found.astype(jnp.int32) - 1
    if step:
        match_ref[...] = jnp.zeros_like(match_ref)


def index_maps(step, snp_index):
    n_blocks = snp_index.shape[1] // BLOCK
    whole = lambda *shape: jax.ShapeDtypeStruct(shape, jnp.int32)
    pos, perm, start, match = pl.pallas_call(
        functools.partial(index_kernel, step),
        out_shape=[
            whole(LANES, LANES),
            whole(n_blocks, TILES, LANES),
            whole(n_blocks, 8, LANES),
            whole(1, snp_index.shape[1] if step == 0 else LANES),
        ],
        compiler_params=pltpu.CompilerParams(vmem_limit_bytes=24 * MIB),
        cost_estimate=estimate(6),
        name="index_maps",
    )(snp_index)
    return pos, perm, start[:, 0, :], match


def pick_lanes(index, sources, first):
    low, high = index & 127, index >> 7
    top, bottom = first
    for number, upper, lower in sources:
        here = high == number
        top = jnp.where(here, jnp.take_along_axis(upper, low, axis=1), top)
        bottom = jnp.where(here, jnp.take_along_axis(lower, low, axis=1), bottom)
    return top, bottom


def tiles_of(ref, base):
    for s in range(ref.shape[1] // LANES):
        span = slice(s * LANES, (s + 1) * LANES)
        yield base + s, ref[0:8, span], ref[8:16, span]


def gather_block(step, block, index_ref, table_ref, store):
    for o in range(TILES):
        span = pl.ds(pl.multiple_of(block * BLOCK + o * LANES, LANES), LANES)
        zero = jnp.zeros((8, LANES), jnp.float32)
        index = jnp.broadcast_to(index_ref[step : step + 1, span], (8, LANES))
        store(o, span, pick_lanes(index, tiles_of(table_ref, 0), (zero, zero)))


def overlay(found, span, spot_ref, match_ref, piece_refs):
    match = jnp.broadcast_to(match_ref[0:1, span], (8, LANES))
    for d, piece_ref in enumerate(piece_refs):
        found = pick_lanes(match, tiles_of(piece_ref, (spot_ref[0] ^ d) * TILES), found)
    return found


def first_kernel(step, index_ref, table_ref, out_ref):
    def store(o, span, found):
        out_ref[0:8, o * LANES : (o + 1) * LANES] = found[0]
        out_ref[8:16, o * LANES : (o + 1) * LANES] = found[1]

    gather_block(step, 0, index_ref, table_ref, store)


def first_block(step, snp_index, table):
    return pl.pallas_call(
        functools.partial(first_kernel, step),
        out_shape=jax.ShapeDtypeStruct((K, BLOCK), jnp.float32),
        compiler_params=pltpu.CompilerParams(vmem_limit_bytes=8 * MIB),
        cost_estimate=estimate(3),
        name="first_block",
    )(snp_index, table)


def em_kernel(step, geno_ref, props_ref, index_ref, table_ref, *refs):
    extra, refs = refs[:-7], refs[-7:]
    sums_ref, num_ref, freq_ref, pt_ref, ps_ref, slots_ref, w_ref = refs
    j = pl.program_id(0)
    last = pl.num_programs(0) - 1
    n_ind = geno_ref.shape[1]
    n_snp = geno_ref.shape[2]

    def store(slot):
        def put(o, span, found):
            if extra:
                spot_ref, _, match_ref, *piece_refs = extra
                found = overlay(found, span, spot_ref, match_ref, piece_refs)
            slots_ref[slot, 0:8, o * LANES : (o + 1) * LANES] = found[0]
            slots_ref[slot, 8:16, o * LANES : (o + 1) * LANES] = found[1]

        return put

    @pl.when(j == 0)
    def _():
        w_ref[...] = scale_of_ind(iota((64, LANES), 0)) * scale_of_snp(iota((64, LANES), 1))
        scaled = props_ref[...] * scale_of_ind(iota((1, n_ind), 1))
        p1, p2, p3 = split3(scaled)
        ps_ref[...] = jnp.concatenate([p1, p2], 0)
        f = lambda v: v.astype(jnp.float32)
        stacked = jnp.concatenate([f(p1), f(p1), f(p2), f(p1), f(p2), f(p3)], 0)
        pt_ref[...] = stacked.T.astype(jnp.bfloat16)
        if extra:
            for o in range(TILES):
                span = slice(o * LANES, (o + 1) * LANES)
                store(0)(o, span, (extra[1][0:8, span], extra[1][8:16, span]))
        else:
            gather_block(step, 0, index_ref, table_ref, store(0))

    slot = lax.rem(j, 2)
    freq = slots_ref[slot]
    freq_ref[...] = freq
    gather_block(step, jnp.minimum(j + 1, last), index_ref, table_ref, store(1 - slot))
    scale_j = scale_of_snp(iota((1, n_snp), 1))
    f1, f2, f3 = split3(freq * scale_j)
    b1, b2, _ = split3((1.0 - freq) * scale_j)
    h = jnp.dot(pt_ref[...], jnp.concatenate([f1, f2, f1, f3, f2, f1], 0), preferred_element_type=jnp.float32)
    w = jnp.concatenate([w_ref[...]] * (n_snp // LANES), 1)
    w = jnp.concatenate([w] * (n_ind // 64), 0)
    inv_a = pl.reciprocal(h, approx=True).astype(jnp.bfloat16)
    inv_b = pl.reciprocal(w - h, approx=True).astype(jnp.bfloat16)
    geno = geno_ref[0]
    ratio_a = geno * inv_a
    ratio_b = (jnp.bfloat16(2) - geno) * inv_b
    ps = ps_ref[...]
    sum_a = jnp.dot(ps, ratio_a, preferred_element_type=jnp.float32)
    sum_b = jnp.dot(ps, ratio_b, preferred_element_type=jnp.float32)
    sums_ref[0, 0:K, :] = sum_a[:K] + sum_a[K:]
    sums_ref[0, K:, :] = sum_b[:K] + sum_b[K:]
    num = lax.dot_general(jnp.concatenate([f1, f2], 0), ratio_a, NT, preferred_element_type=jnp.float32)
    num += lax.dot_general(jnp.concatenate([b1, b2], 0), ratio_b, NT, preferred_element_type=jnp.float32)
    num = num[:K] + num[K:]

    @pl.when(j == 0)
    def _():
        num_ref[...] = num

    @pl.when(j != 0)
    def _():
        num_ref[...] += num


def em_sums(step, genotypes, props, snp_index, table, extra):
    n_ind, n_snp = genotypes.shape[1:]
    fixed = lambda j: (0, 0)
    whole = lambda a: pl.BlockSpec(a.shape, fixed)
    specs = [pl.BlockSpec(memory_space=pltpu.SMEM), *map(whole, extra[1:])] if extra else []
    return pl.pallas_call(
        functools.partial(em_kernel, step),
        grid=(n_snp // BLOCK,),
        in_specs=[
            pl.BlockSpec((1, n_ind, BLOCK), lambda j: (step, 0, j)),
            whole(props),
            whole(snp_index),
            whole(table),
            *specs,
        ],
        out_specs=[
            pl.BlockSpec((1, 2 * K, BLOCK), lambda j: (j, 0, 0)),
            pl.BlockSpec((K, n_ind), fixed),
            pl.BlockSpec((K, BLOCK), lambda j: (0, j)),
        ],
        out_shape=[
            jax.ShapeDtypeStruct((n_snp // BLOCK, 2 * K, BLOCK), jnp.float32),
            jax.ShapeDtypeStruct((K, n_ind), jnp.float32),
            jax.ShapeDtypeStruct((K, n_snp), jnp.float32),
        ],
        scratch_shapes=[
            pltpu.VMEM((n_ind, 6 * K), jnp.bfloat16),
            pltpu.VMEM((2 * K, n_ind), jnp.bfloat16),
            pltpu.VMEM((2, K, BLOCK), jnp.float32),
            pltpu.VMEM((64, LANES), jnp.float32),
        ],
        compiler_params=pltpu.CompilerParams(vmem_limit_bytes=(40 if extra else 62) * MIB),
        cost_estimate=estimate(18),
        name="em_sums",
    )(genotypes, props, snp_index, table, *extra)


def finish_kernel(mine_ref, other_ref, old_ref, perm_ref, new_ref, hold_ref):
    sums = mine_ref[...] + other_ref[...]
    old = old_ref[...]
    acc_a = old * sums[:K]
    acc_b = (1.0 - old) * sums[K:]
    hold_ref[...] = acc_a / (acc_a + acc_b)
    for o in range(TILES):
        index = jnp.broadcast_to(perm_ref[o : o + 1, :], (8, LANES))
        zero = jnp.zeros((8, LANES), jnp.float32)
        top, bottom = pick_lanes(index, tiles_of(hold_ref, 0), (zero, zero))
        new_ref[0:8, o * LANES : (o + 1) * LANES] = top
        new_ref[8:16, o * LANES : (o + 1) * LANES] = bottom


def finish(mine, other, old, perm):
    return pl.pallas_call(
        finish_kernel,
        out_shape=jax.ShapeDtypeStruct(old.shape, jnp.float32),
        scratch_shapes=[pltpu.VMEM(old.shape, jnp.float32)],
        compiler_params=pltpu.CompilerParams(vmem_limit_bytes=4 * MIB),
        cost_estimate=estimate(1),
        name="finish",
    )(mine, other, old, perm)


def place_kernel(spot_ref, start_ref, pos_ref, table_ref, *refs):
    piece_refs, out_ref = refs[:-1], refs[-1]
    rows = pos_ref.shape[0]
    first = pl.program_id(0) * rows
    for o in range(rows):
        span = slice(o * LANES, (o + 1) * LANES)
        index = jnp.broadcast_to(pos_ref[o : o + 1, :], (8, LANES))
        found = (table_ref[0:8, span], table_ref[8:16, span])
        for d, piece_ref in enumerate(piece_refs):
            piece = spot_ref[0] ^ d
            tile = start_ref[piece, first + o]
            sources = []
            for step in range(2):
                here = pl.ds(pl.multiple_of((tile + step) * LANES, LANES), LANES)
                sources.append((piece * TILES + tile + step, piece_ref[0:8, here], piece_ref[8:16, here]))
            found = pick_lanes(index, sources, found)
        out_ref[0:8, span] = found[0]
        out_ref[8:16, span] = found[1]


def place(table, pieces, pos, start, spot):
    rows = 32
    fixed = lambda i: (0, 0)
    return pl.pallas_call(
        place_kernel,
        grid=(pos.shape[0] // rows,),
        in_specs=[
            pl.BlockSpec(memory_space=pltpu.SMEM),
            pl.BlockSpec(memory_space=pltpu.SMEM),
            pl.BlockSpec((rows, LANES), lambda i: (i, 0)),
            pl.BlockSpec((K, rows * LANES), lambda i: (0, i)),
            *[pl.BlockSpec(p.shape, fixed) for p in pieces],
        ],
        out_specs=pl.BlockSpec((K, rows * LANES), lambda i: (0, i)),
        out_shape=jax.ShapeDtypeStruct(table.shape, jnp.float32),
        compiler_params=pltpu.CompilerParams(vmem_limit_bytes=16 * MIB),
        cost_estimate=estimate(5),
        name="place",
    )(spot, start, pos, table, *pieces)


def swap(value, axis, bits):
    size = lax.axis_size(axis)
    return lax.ppermute(value, axis, [(i, i ^ bits) for i in range(size)])


def all_sum4(value, axis, unit):
    one, two, three = (swap(value, axis, d * unit) for d in (1, 2, 3))
    return (value + one) + (two + three)


def together(*values):
    return lax.optimization_barrier(values)


def per_device(genotypes, snp_index, props, freq_table):
    batch_total = genotypes.shape[2] * lax.axis_size("snp")
    n_ind = genotypes.shape[1]
    spot = lax.axis_index("ind") // 8
    spot_array = jnp.reshape(spot, (1,)).astype(jnp.int32)
    table, extra = freq_table, ()
    for step in range(STEPS):
        sums, num, freq = em_sums(step, genotypes, props, snp_index, freq_table, extra)
        if step == 0:
            indexes, _ = together(snp_index, num)
            in_x = lambda: index_maps(0, indexes)
            in_y = lambda: first_block(1, indexes, freq_table)
        else:
            held, _ = together((freq_table, snp_index), num)
            in_x = lambda: place(held[0], pieces, maps[0], maps[2], spot_array)
            in_y = lambda: index_maps(1, held[1])
        block = lambda d: lax.dynamic_index_in_dim(sums, spot ^ d, 0, False)
        parts = [swap(block(d), "ind", 8 * d) for d in (1, 2, 3)]
        mine = (block(0) + parts[0]) + (parts[1] + parts[2])
        mine, from_x = together(mine, in_x())
        mine = all_sum4(mine, "ind", 2)
        mine, from_y = together(mine, in_y())
        if step == 0:
            maps, first = from_x, from_y
        else:
            table, maps = from_x, from_y
        old = lax.dynamic_slice_in_dim(freq, spot * BLOCK, BLOCK, 1)
        new = finish(mine, swap(mine, "ind", 1), old, lax.dynamic_index_in_dim(maps[1], spot, 0, False))
        pieces = [new] + [swap(new, "ind", 8 * d) for d in (1, 2, 3)]
        if step == 0:
            extra = (spot_array, first, maps[3], *pieces)
        prop_num = all_sum4(num, "snp", 1)
        scale_i = scale_of_ind(jnp.arange(n_ind))
        props = props * (prop_num * scale_i) / (2.0 * batch_total)
    return (jnp.log(props), place(table, pieces, maps[0], maps[2], spot_array))


def solution(mesh):
    placed = (P(None, "ind", "snp"), P(None, "snp"), P(None, "ind"), P(None, "snp"))
    return jax.shard_map(
        per_device,
        mesh=mesh,
        in_specs=placed,
        out_specs=(P(None, "ind"), P(None, "snp")),
        check_vma=False,
    )
```

```python
import functools

import jax
import jax.numpy as jnp
import numpy as np
from jax import lax
from jax.experimental import pallas as pl
from jax.experimental.pallas import tpu as pltpu
from jax.sharding import PartitionSpec as P

STEPS = 2
K = 16
LANES = 128
BLOCK = 1024
TILES = BLOCK // LANES
NN = (((1,), (0,)), ((), ()))
NT = (((1,), (1,)), ((), ()))
TN = (((0,), (0,)), ((), ()))
MIB = 1 << 20

def scale_of_ind(i):
    return ((i % 64 * 37 + 5) % 128 + 128).astype(jnp.float32) * (1.0 / 256)


def scale_of_snp(j):
    return ((j % 128 * 53 + 11) % 128 + 128).astype(jnp.float32) * (1.0 / 256)


def iota(shape, dim):
    return lax.broadcasted_iota(jnp.int32, shape, dim)


def estimate(us):
    return pl.CostEstimate(flops=0, bytes_accessed=int(us * 3.5e6), transcendentals=0)


def split3(x):
    one = x.astype(jnp.bfloat16)
    rest = x - one.astype(jnp.float32)
    two = rest.astype(jnp.bfloat16)
    three = (rest - two.astype(jnp.float32)).astype(jnp.bfloat16)
    return one, two, three


def dot_exact(left, right, dims):
    return lax.dot_general(
        left.astype(jnp.bfloat16), right.astype(jnp.bfloat16), dims, preferred_element_type=jnp.float32
    )


def one_hot(count, value):
    ids = lax.broadcasted_iota(jnp.int32, (count, value.shape[1]), 0)
    return (ids == value).astype(jnp.float32).astype(jnp.bfloat16)


def halves(x):
    hi = jnp.floor(x * (1.0 / LANES))
    return hi, x - LANES * hi


def look_up(table, hot_hi, hot_lo):
    hi, lo = halves(table)
    pick = hot_lo.astype(jnp.float32)
    first = jnp.sum(pick * dot_exact(hi, hot_hi, TN), 0, keepdims=True)
    return LANES * first + jnp.sum(pick * dot_exact(lo, hot_hi, TN), 0, keepdims=True)


def index_kernel(step, blocks, rows_ref, *refs):
    before_refs, (pos_ref, perm_ref, start_ref, *match_refs) = refs[: min(blocks[0], 1)], refs[min(blocks[0], 1) :]
    row = lax.broadcasted_iota(jnp.int32, (LANES, LANES), 0)
    col = lax.broadcasted_iota(jnp.int32, (LANES, LANES), 1)
    below = (col < row).astype(jnp.float32)
    above = (row < col).astype(jnp.float32)
    ones = jnp.ones((LANES, LANES), jnp.float32)
    local = lax.broadcasted_iota(jnp.int32, (1, BLOCK), 1).astype(jnp.float32)
    local_hi, local_lo = (v.astype(jnp.bfloat16) for v in halves(local))
    pos = before_refs[0][...].astype(jnp.float32) if before_refs else jnp.full((LANES, LANES), -1.0, jnp.float32)
    for place, b in enumerate(blocks):
        rows = rows_ref[step : step + 1, b * BLOCK : (b + 1) * BLOCK]
        hot_hi, hot_lo = one_hot(LANES, rows >> 7), one_hot(LANES, rows & 127)
        mask = dot_exact(hot_hi, hot_lo, NT)
        rank = dot_exact(dot_exact(below, mask, NN), ones, NN) + dot_exact(mask, above, NN)
        counts = dot_exact(jnp.ones((16, BLOCK), jnp.float32), hot_hi, NT)
        before = dot_exact(counts, above, NN)[:8].astype(jnp.int32)
        start_ref[place] = before
        pos = jnp.where(mask > 0.5, rank + float(b * BLOCK), pos)
        rank_j = look_up(rank, hot_hi, hot_lo).astype(jnp.int32)
        hot_rank = one_hot(16, rank_j >> 7)
        hot_low = one_hot(LANES, rank_j & 127)
        perm = LANES * dot_exact(hot_rank * local_hi, hot_low, NT) + dot_exact(hot_rank * local_lo, hot_low, NT)
        perm_ref[place] = perm[:TILES].astype(jnp.int32)
    pos_ref[...] = pos.astype(jnp.int32)
    for match_ref in match_refs:
        for b in range(match_ref.shape[1] // BLOCK):
            span = slice(b * BLOCK, (b + 1) * BLOCK)
            rows = rows_ref[1:2, span]
            found = look_up(pos + 1.0, one_hot(LANES, rows >> 7), one_hot(LANES, rows & 127))
            match_ref[0:1, span] = found.astype(jnp.int32) - 1


def index_part(step, blocks, snp_index, before=()):
    n_snp = snp_index.shape[1]
    whole = lambda *shape: jax.ShapeDtypeStruct(shape, jnp.int32)
    last = blocks[-1] == n_snp // BLOCK - 1
    outs = [whole(LANES, LANES), whole(len(blocks), TILES, LANES), whole(len(blocks), 8, LANES)]
    return pl.pallas_call(
        functools.partial(index_kernel, step, blocks),
        out_shape=outs + ([whole(1, n_snp)] if last and step == 0 else []),
        compiler_params=pltpu.CompilerParams(vmem_limit_bytes=24 * MIB),
        cost_estimate=estimate(3),
        name="index_part",
    )(snp_index, *before)


def pick_lanes(index, sources, first):
    low, high = index & 127, index >> 7
    top, bottom = first
    for number, upper, lower in sources:
        here = high == number
        top = jnp.where(here, jnp.take_along_axis(upper, low, axis=1), top)
        bottom = jnp.where(here, jnp.take_along_axis(lower, low, axis=1), bottom)
    return top, bottom


def tiles_of(ref, base):
    for s in range(ref.shape[1] // LANES):
        span = slice(s * LANES, (s + 1) * LANES)
        yield base + s, ref[0:8, span], ref[8:16, span]


def put(ref, o, found):
    ref[0:8, o * LANES : (o + 1) * LANES] = found[0]
    ref[8:16, o * LANES : (o + 1) * LANES] = found[1]


def gather_tile(step, block, o, index_ref, table_ref):
    span = pl.ds(pl.multiple_of(block * BLOCK + o * LANES, LANES), LANES)
    zero = jnp.zeros((8, LANES), jnp.float32)
    index = jnp.broadcast_to(index_ref[step : step + 1, span], (8, LANES))
    return pick_lanes(index, tiles_of(table_ref, 0), (zero, zero)), span


def overlay(found, span, spot, match_ref, piece_refs):
    match = jnp.broadcast_to(match_ref[0:1, span], (8, LANES))
    for d, piece_ref in enumerate(piece_refs):
        found = pick_lanes(match, tiles_of(piece_ref, (spot ^ d) * TILES), found)
    return found


def first_kernel(step, spot_ref, index_ref, table_ref, out_ref):
    for o in range(TILES):
        put(out_ref, o, gather_tile(step, spot_ref[0] ^ 1, o, index_ref, table_ref)[0])


def first_block(step, spot, snp_index, table):
    vmem = pl.BlockSpec(memory_space=pltpu.VMEM)
    return pl.pallas_call(
        functools.partial(first_kernel, step),
        in_specs=[pl.BlockSpec(memory_space=pltpu.SMEM), vmem, vmem],
        out_shape=jax.ShapeDtypeStruct((K, BLOCK), jnp.float32),
        compiler_params=pltpu.CompilerParams(vmem_limit_bytes=8 * MIB),
        cost_estimate=estimate(3),
        name="first_block",
    )(spot, snp_index, table)


def geno_copy(step, block, geno_hbm, geno_ref, sem):
    span = pl.ds(pl.multiple_of(block * BLOCK, BLOCK), BLOCK)
    return pltpu.make_async_copy(geno_hbm.at[step, :, span], geno_ref, sem)


def block_sums(step, geno, freq, pt_ref, ps_ref, w_ref):
    n_ind, n_snp = geno.shape
    scale_j = scale_of_snp(iota((1, n_snp), 1))
    f1, f2, f3 = split3(freq * scale_j)
    b1, b2, _ = split3((1.0 - freq) * scale_j)
    h = jnp.dot(pt_ref[...], jnp.concatenate([f1, f2, f1, f3, f2, f1], 0), preferred_element_type=jnp.float32)
    w = jnp.concatenate([w_ref[...]] * (n_snp // LANES), 1)
    w = jnp.concatenate([w] * (n_ind // 64), 0)
    inv_a = pl.reciprocal(h, approx=True).astype(jnp.bfloat16)
    inv_b = pl.reciprocal(w - h, approx=True).astype(jnp.bfloat16)
    ratio_a = geno * inv_a
    ratio_b = (jnp.bfloat16(2) - geno) * inv_b
    ps = ps_ref[...]
    sum_a = jnp.dot(ps, ratio_a, preferred_element_type=jnp.float32)
    sum_b = jnp.dot(ps, ratio_b, preferred_element_type=jnp.float32)
    first = ratio_a - ratio_b if step == 0 else ratio_a
    num = lax.dot_general(jnp.concatenate([f1, f2], 0), first, NT, preferred_element_type=jnp.float32)
    if step:
        num += lax.dot_general(jnp.concatenate([b1, b2], 0), ratio_b, NT, preferred_element_type=jnp.float32)
    return sum_a[:K] + sum_a[K:], sum_b[:K] + sum_b[K:], num[:K] + num[K:]


def set_scales(w_ref):
    w_ref[...] = scale_of_ind(iota((64, LANES), 0)) * scale_of_snp(iota((64, LANES), 1))


def split_props(props, pt_ref, ps_ref):
    scaled = props * scale_of_ind(iota((1, props.shape[1]), 1))
    p1, p2, p3 = split3(scaled)
    ps_ref[...] = jnp.concatenate([p1, p2], 0)
    f = lambda v: v.astype(jnp.float32)
    stacked = jnp.concatenate([f(p1), f(p1), f(p2), f(p1), f(p2), f(p3)], 0)
    pt_ref[...] = stacked.T.astype(jnp.bfloat16)


def prepare_kernel(step, spot_ref, geno_hbm, props_ref, pt_ref, ps_ref, near_ref, own_ref, sems):
    spot = spot_ref[0]
    near = geno_copy(step, spot ^ 1, geno_hbm, near_ref, sems.at[0])
    own = geno_copy(step, spot, geno_hbm, own_ref, sems.at[1])
    near.start()
    own.start()
    split_props(props_ref[...], pt_ref, ps_ref)
    near.wait()
    own.wait()


def prepare(step, spot, genotypes, props):
    n_ind = genotypes.shape[1]
    smem, vmem = (pl.BlockSpec(memory_space=space) for space in (pltpu.SMEM, pltpu.VMEM))
    shape = lambda a, b: jax.ShapeDtypeStruct((a, b), jnp.bfloat16)
    return pl.pallas_call(
        functools.partial(prepare_kernel, step),
        in_specs=[smem, pl.BlockSpec(memory_space=pl.ANY), vmem],
        out_specs=[vmem] * 4,
        out_shape=[shape(n_ind, 6 * K), shape(2 * K, n_ind), shape(n_ind, BLOCK), shape(n_ind, BLOCK)],
        scratch_shapes=[pltpu.SemaphoreType.DMA((2,))],
        compiler_params=pltpu.CompilerParams(vmem_limit_bytes=47 * MIB),
        cost_estimate=estimate(2),
        name="prepare",
    )(spot, genotypes, props)


def far_kernel(step, spot_ref, geno_hbm, props_ref, index_ref, table_ref, *refs):
    if step:
        pt_ref, ps_ref, near_ref, first_ref, match_ref, *piece_refs = refs[:-9]
        *sums_refs, num_ref, own_ref, freq_ref, w_ref, geno_ref, sems = refs[-9:]
    else:
        *sums_refs, num_ref, own_ref, pt_ref, ps_ref, freq_ref, w_ref, geno_ref, sems = refs
    spot = spot_ref[0]
    fetch = lambda d: geno_copy(step, spot ^ d, geno_hbm, geno_ref.at[d - 1], sems.at[d - 1])

    def gather(d, half):
        for o in range(half * TILES // 2, (half + 1) * TILES // 2):
            if step and d == 1:
                here = slice(o * LANES, (o + 1) * LANES)
                found = (first_ref[0:8, here], first_ref[8:16, here])
                span = pl.ds(pl.multiple_of((spot ^ d) * BLOCK + o * LANES, LANES), LANES)
            else:
                found, span = gather_tile(step, spot ^ d, o, index_ref, table_ref)
            if step:
                found = overlay(found, span, spot, match_ref, piece_refs)
            put(freq_ref.at[d - 1] if d else own_ref, o, found)

    fetched = (2, 3) if step else (1, 2, 3)
    fetch(fetched[0]).start()
    set_scales(w_ref)
    if not step:
        split_props(props_ref[...], pt_ref, ps_ref)
    gather(1, 0)
    total = jnp.zeros(num_ref.shape, jnp.float32)
    order = [(d, half) for d in (1, 2, 3, 0) for half in (0, 1)]
    for (d, half), following in zip(order[:6], order[1:7]):
        if half == 0 and d in fetched:
            fetch(d).wait()
            if d < 3:
                fetch(d + 1).start()
        gather(*following)
        cols = slice(half * BLOCK // 2, (half + 1) * BLOCK // 2)
        geno = near_ref[:, cols] if step and d == 1 else geno_ref[d - 1, :, cols]
        sum_a, sum_b, num = block_sums(step, geno, freq_ref[d - 1, :, cols], pt_ref, ps_ref, w_ref)
        sums_refs[d - 1][0:K, cols] = sum_a
        sums_refs[d - 1][K:, cols] = sum_b
        total += num
    gather(0, 1)
    num_ref[...] = total


def far_sums(step, spot, genotypes, props, snp_index, table, extra):
    n_ind, n_snp = genotypes.shape[1:]
    assert n_snp == 4 * BLOCK
    smem, vmem = (pl.BlockSpec(memory_space=space) for space in (pltpu.SMEM, pltpu.VMEM))
    shape = lambda a, b, t=jnp.float32: jax.ShapeDtypeStruct((a, b), t)
    outs = [
        *[shape(2 * K, BLOCK)] * 3,
        shape(K, n_ind),
        shape(K, BLOCK),
    ]
    if step == 0:
        outs += [shape(n_ind, 6 * K, jnp.bfloat16), shape(2 * K, n_ind, jnp.bfloat16)]
    return pl.pallas_call(
        functools.partial(far_kernel, step),
        in_specs=[smem, pl.BlockSpec(memory_space=pl.ANY), *[vmem] * (3 + len(extra))],
        out_specs=[vmem] * len(outs),
        scratch_shapes=[
            pltpu.VMEM((3, K, BLOCK), jnp.float32),
            pltpu.VMEM((64, LANES), jnp.float32),
            pltpu.VMEM((3, n_ind, BLOCK), jnp.bfloat16),
            pltpu.SemaphoreType.DMA((3,)),
        ],
        out_shape=outs,
        compiler_params=pltpu.CompilerParams(vmem_limit_bytes=(40 if step else 62) * MIB),
        cost_estimate=estimate(14),
        name="far_sums",
    )(spot, genotypes, props, snp_index, table, *extra)


def own_kernel(step, spot_ref, geno_ref, freq_ref, pt_ref, ps_ref, before_ref, sums_ref, num_ref, w_ref):
    set_scales(w_ref)
    geno = geno_ref[...] if step else geno_ref[0]
    sum_a, sum_b, num = block_sums(step, geno, freq_ref[...], pt_ref, ps_ref, w_ref)
    sums_ref[0:K, :] = sum_a
    sums_ref[K:, :] = sum_b
    num_ref[...] = before_ref[...] + num


def own_sums(step, spot, geno, freq, pt, ps, before):
    n_ind = pt.shape[0]
    outs = [jax.ShapeDtypeStruct((2 * K, BLOCK), jnp.float32), jax.ShapeDtypeStruct(before.shape, jnp.float32)]
    scratch = [pltpu.VMEM((64, LANES), jnp.float32)]
    if step:
        smem, vmem = (pl.BlockSpec(memory_space=space) for space in (pltpu.SMEM, pltpu.VMEM))
        layout = dict(in_specs=[smem] + [vmem] * 5, out_specs=[vmem] * 2, scratch_shapes=scratch)
    else:
        fixed = lambda j, s: (0, 0)
        layout = dict(
            grid_spec=pltpu.PrefetchScalarGridSpec(
                num_scalar_prefetch=1,
                grid=(1,),
                in_specs=[
                    pl.BlockSpec((1, n_ind, BLOCK), lambda j, s: (step, 0, s[0])),
                    *[pl.BlockSpec(a.shape, fixed) for a in (freq, pt, ps, before)],
                ],
                out_specs=[pl.BlockSpec(a.shape, fixed) for a in outs],
                scratch_shapes=scratch,
            )
        )
    return pl.pallas_call(
        functools.partial(own_kernel, step),
        out_shape=outs,
        compiler_params=pltpu.CompilerParams(vmem_limit_bytes=(40 if step else 62) * MIB),
        cost_estimate=estimate(5),
        name="own_sums",
        **layout,
    )(spot, geno, freq, pt, ps, before)


def finish_kernel(mine_ref, other_ref, old_ref, perm_ref, new_ref, hold_ref):
    sums = mine_ref[...] + other_ref[...]
    old = old_ref[...]
    acc_a = old * sums[:K]
    acc_b = (1.0 - old) * sums[K:]
    hold_ref[...] = acc_a / (acc_a + acc_b)
    for o in range(TILES):
        index = jnp.broadcast_to(perm_ref[o : o + 1, :], (8, LANES))
        zero = jnp.zeros((8, LANES), jnp.float32)
        top, bottom = pick_lanes(index, tiles_of(hold_ref, 0), (zero, zero))
        put(new_ref, o, (top, bottom))


def finish(mine, other, old, perm):
    return pl.pallas_call(
        finish_kernel,
        out_shape=jax.ShapeDtypeStruct(old.shape, jnp.float32),
        scratch_shapes=[pltpu.VMEM(old.shape, jnp.float32)],
        compiler_params=pltpu.CompilerParams(vmem_limit_bytes=4 * MIB),
        cost_estimate=estimate(1),
        name="finish",
    )(mine, other, old, perm)


def place_kernel(spot_ref, start_ref, pos_ref, table_ref, *refs):
    piece_refs, out_ref = refs[:-1], refs[-1]
    rows = pos_ref.shape[0]
    first = pl.program_id(0) * rows
    lane = iota((8, LANES), 1)
    for o in range(rows):
        span = slice(o * LANES, (o + 1) * LANES)
        pos = jnp.broadcast_to(pos_ref[o : o + 1, :], (8, LANES))
        low, owner = pos & 127, pos >> 10
        top, bottom = table_ref[0:8, span], table_ref[8:16, span]
        for d, piece_ref in enumerate(piece_refs):
            piece = spot_ref[0] ^ d
            before = start_ref[piece, first + o]
            tile = jnp.minimum(before >> 7, TILES - 1)
            ends = [pl.ds(pl.multiple_of(t * LANES, LANES), LANES) for t in (tile, jnp.minimum(tile + 1, TILES - 1))]
            head = lane >= (before & 127)
            upper = jnp.where(head, piece_ref[0:8, ends[0]], piece_ref[0:8, ends[1]])
            lower = jnp.where(head, piece_ref[8:16, ends[0]], piece_ref[8:16, ends[1]])
            here = owner == piece
            top = jnp.where(here, jnp.take_along_axis(upper, low, axis=1), top)
            bottom = jnp.where(here, jnp.take_along_axis(lower, low, axis=1), bottom)
        put(out_ref, o, (top, bottom))


def place(table, pieces, pos, start, spot):
    rows = 32
    fixed = lambda i: (0, 0)
    return pl.pallas_call(
        place_kernel,
        grid=(pos.shape[0] // rows,),
        in_specs=[
            pl.BlockSpec(memory_space=pltpu.SMEM),
            pl.BlockSpec(memory_space=pltpu.SMEM),
            pl.BlockSpec((rows, LANES), lambda i: (i, 0)),
            pl.BlockSpec((K, rows * LANES), lambda i: (0, i)),
            *[pl.BlockSpec(p.shape, fixed) for p in pieces],
        ],
        out_specs=pl.BlockSpec((K, rows * LANES), lambda i: (0, i)),
        out_shape=jax.ShapeDtypeStruct(table.shape, jnp.float32),
        compiler_params=pltpu.CompilerParams(vmem_limit_bytes=16 * MIB),
        cost_estimate=estimate(4),
        name="place",
    )(spot, start, pos, table, *pieces)


def swap(value, axis, bits):
    size = lax.axis_size(axis)
    return lax.ppermute(value, axis, [(i, i ^ bits) for i in range(size)])


def all_sum4(value, axis, unit):
    one, two, three = (swap(value, axis, d * unit) for d in (1, 2, 3))
    return (value + one) + (two + three)


def together(*values):
    return lax.optimization_barrier(values)


def per_device(genotypes, snp_index, props, freq_table):
    batch_total = genotypes.shape[2] * lax.axis_size("snp")
    n_ind = genotypes.shape[1]
    spot = lax.axis_index("ind") // 8
    spot_array = jnp.reshape(spot, (1,)).astype(jnp.int32)
    extra = ()
    for step in range(STEPS):
        *far, num, old = far_sums(step, spot_array, genotypes, props, snp_index, freq_table, extra)
        if step == 0:
            *far, num, old, pt, ps = *far, num, old
            geno_own = genotypes
        parts = [swap(far[d - 1], "ind", 8 * d) for d in (1, 2, 3)]
        mine, num = own_sums(step, spot_array, geno_own, old, pt, ps, num)
        mine = (mine + parts[0]) + (parts[1] + parts[2])
        mine, held, indexes = together(mine, freq_table, snp_index)
        mine = all_sum4(mine, "ind", 2)
        across = swap(num, "snp", 1)
        pos, perm_a, start_a = index_part(step, (0, 1), indexes)
        num, across, pos = together(num, across, pos)
        num = num + across
        num, pos = together(num, pos)
        num = num + swap(num, "snp", 2)
        pos, perm_b, start_b, *match = index_part(step, (2, 3), indexes, (pos,))
        perm = jnp.concatenate([perm_a, perm_b])
        start = jnp.concatenate([start_a[:, 0], start_b[:, 0]])
        other = swap(mine, "ind", 1)
        mine, held, indexes = together(mine, freq_table, snp_index)
        if step == 0:
            beside = first_block(1, spot_array, indexes, held)
        else:
            beside = place(held, pieces, *maps, spot_array)
        other, beside = together(other, beside)
        maps = (pos, start)
        new = finish(mine, other, old, lax.dynamic_index_in_dim(perm, spot, 0, False))
        pieces = [new] + [swap(new, "ind", 8 * d) for d in (1, 2, 3)]
        prop_num = num * scale_of_ind(jnp.arange(n_ind))
        if step == 0:
            prop_num = 2.0 * batch_total + (prop_num - jnp.sum(props * prop_num, 0, keepdims=True))
        props = props * prop_num / (2.0 * batch_total)
        if step == 0:
            pt, ps, near, geno_own = prepare(1, spot_array, genotypes, together(props, new)[0])
            extra = (pt, ps, near, beside, *match, *pieces)
    return (jnp.log(props), place(beside, pieces, *maps, spot_array))


def solution(mesh):
    placed = (P(None, "ind", "snp"), P(None, "snp"), P(None, "ind"), P(None, "snp"))
    return jax.shard_map(
        per_device,
        mesh=mesh,
        in_specs=placed,
        out_specs=(P(None, "ind"), P(None, "snp")),
        check_vma=False,
    )
```

```python
import functools

import jax
import jax.numpy as jnp
import numpy as np
from jax import lax
from jax.experimental import pallas as pl
from jax.experimental.pallas import tpu as pltpu
from jax.sharding import PartitionSpec as P

STEPS = 2
K = 16
LANES = 128
BLOCK = 1024
TILES = BLOCK // LANES
HALF = BLOCK // 2
NN = (((1,), (0,)), ((), ()))
NT = (((1,), (1,)), ((), ()))
TN = (((0,), (0,)), ((), ()))
MIB = 1 << 20

def scale_of_ind(i):
    return ((i % 64 * 37 + 5) % 128 + 128).astype(jnp.float32) * (1.0 / 256)


def scale_of_snp(j):
    return ((j % 128 * 53 + 11) % 128 + 128).astype(jnp.float32) * (1.0 / 256)


def iota(shape, dim):
    return lax.broadcasted_iota(jnp.int32, shape, dim)


def estimate(us):
    return pl.CostEstimate(flops=0, bytes_accessed=int(us * 3.5e6), transcendentals=0)


def split3(x):
    one = x.astype(jnp.bfloat16)
    rest = x - one.astype(jnp.float32)
    two = rest.astype(jnp.bfloat16)
    three = (rest - two.astype(jnp.float32)).astype(jnp.bfloat16)
    return one, two, three


def dot_exact(left, right, dims):
    return lax.dot_general(
        left.astype(jnp.bfloat16), right.astype(jnp.bfloat16), dims, preferred_element_type=jnp.float32
    )


def one_hot(count, value):
    ids = lax.broadcasted_iota(jnp.int32, (count, value.shape[1]), 0)
    return (ids == value).astype(jnp.float32).astype(jnp.bfloat16)


def halves(x):
    hi = jnp.floor(x * (1.0 / LANES))
    return hi, x - LANES * hi


def look_up(table, hot_hi, hot_lo):
    hi, lo = halves(table)
    pick = hot_lo.astype(jnp.float32)
    first = jnp.sum(pick * dot_exact(hi, hot_hi, TN), 0, keepdims=True)
    return LANES * first + jnp.sum(pick * dot_exact(lo, hot_hi, TN), 0, keepdims=True)


def index_kernel(step, blocks, rows_ref, *refs):
    before_refs, (pos_ref, perm_ref, start_ref, *match_refs) = refs[: min(blocks[0], 1)], refs[min(blocks[0], 1) :]
    row = lax.broadcasted_iota(jnp.int32, (LANES, LANES), 0)
    col = lax.broadcasted_iota(jnp.int32, (LANES, LANES), 1)
    below = (col < row).astype(jnp.float32)
    above = (row < col).astype(jnp.float32)
    ones = jnp.ones((LANES, LANES), jnp.float32)
    local = lax.broadcasted_iota(jnp.int32, (1, BLOCK), 1).astype(jnp.float32)
    local_hi, local_lo = (v.astype(jnp.bfloat16) for v in halves(local))
    pos = before_refs[0][...].astype(jnp.float32) if before_refs else jnp.full((LANES, LANES), -1.0, jnp.float32)
    span_of = lambda b: pl.ds(pl.multiple_of(b * BLOCK, BLOCK), BLOCK)

    def one_block(b, pos):
        rows = rows_ref[step : step + 1, span_of(b)]
        hot_hi, hot_lo = one_hot(LANES, rows >> 7), one_hot(LANES, rows & 127)
        mask = dot_exact(hot_hi, hot_lo, NT)
        rank = dot_exact(dot_exact(below, mask, NN), ones, NN) + dot_exact(mask, above, NN)
        counts = dot_exact(jnp.ones((16, BLOCK), jnp.float32), hot_hi, NT)
        start_ref[b - blocks[0]] = dot_exact(counts, above, NN)[:8].astype(jnp.int32)
        rank_j = look_up(rank, hot_hi, hot_lo).astype(jnp.int32)
        hot_rank = one_hot(16, rank_j >> 7)
        hot_low = one_hot(LANES, rank_j & 127)
        perm = LANES * dot_exact(hot_rank * local_hi, hot_low, NT) + dot_exact(hot_rank * local_lo, hot_low, NT)
        perm_ref[b - blocks[0]] = perm[:TILES].astype(jnp.int32)
        return jnp.where(mask > 0.5, rank + (b * BLOCK).astype(jnp.float32), pos)

    pos = lax.fori_loop(blocks[0], blocks[-1] + 1, one_block, pos)
    pos_ref[...] = pos.astype(jnp.int32)
    for match_ref in match_refs:

        def one_match(b, _, match_ref=match_ref):
            rows = rows_ref[1:2, span_of(b)]
            found = look_up(pos + 1.0, one_hot(LANES, rows >> 7), one_hot(LANES, rows & 127))
            match_ref[0:1, span_of(b)] = found.astype(jnp.int32) - 1
            return 0

        lax.fori_loop(0, match_ref.shape[1] // BLOCK, one_match, 0)


def index_part(step, blocks, snp_index, before=()):
    n_snp = snp_index.shape[1]
    whole = lambda *shape: jax.ShapeDtypeStruct(shape, jnp.int32)
    last = blocks[-1] == n_snp // BLOCK - 1
    outs = [whole(LANES, LANES), whole(len(blocks), TILES, LANES), whole(len(blocks), 8, LANES)]
    return pl.pallas_call(
        functools.partial(index_kernel, step, blocks),
        out_shape=outs + ([whole(1, n_snp)] if last and step == 0 else []),
        compiler_params=pltpu.CompilerParams(vmem_limit_bytes=24 * MIB),
        cost_estimate=estimate(3),
        name="index_part",
    )(snp_index, *before)


def pick_lanes(index, sources, first):
    low, high = index & 127, index >> 7
    top, bottom = first
    for number, upper, lower in sources:
        here = high == number
        top = jnp.where(here, jnp.take_along_axis(upper, low, axis=1), top)
        bottom = jnp.where(here, jnp.take_along_axis(lower, low, axis=1), bottom)
    return top, bottom


def tiles_of(ref, base):
    for s in range(ref.shape[1] // LANES):
        span = slice(s * LANES, (s + 1) * LANES)
        yield base + s, ref[0:8, span], ref[8:16, span]


def put(ref, o, found):
    ref[0:8, o * LANES : (o + 1) * LANES] = found[0]
    ref[8:16, o * LANES : (o + 1) * LANES] = found[1]


def gather_tile(step, block, o, index_ref, table_ref):
    span = pl.ds(pl.multiple_of(block * BLOCK + o * LANES, LANES), LANES)
    zero = jnp.zeros((8, LANES), jnp.float32)
    index = jnp.broadcast_to(index_ref[step : step + 1, span], (8, LANES))
    return pick_lanes(index, tiles_of(table_ref, 0), (zero, zero)), span


def overlay(found, span, spot, match_ref, piece_refs):
    match = jnp.broadcast_to(match_ref[0:1, span], (8, LANES))
    for d, piece_ref in enumerate(piece_refs):
        found = pick_lanes(match, tiles_of(piece_ref, (spot ^ d) * TILES), found)
    return found


def first_kernel(step, spot_ref, index_ref, table_ref, out_ref):
    def some_tiles(i, _):
        for o in (2 * i, 2 * i + 1):
            found, _ = gather_tile(step, spot_ref[0] ^ 1, o, index_ref, table_ref)
            here = pl.ds(pl.multiple_of(o * LANES, LANES), LANES)
            out_ref[0:8, here], out_ref[8:16, here] = found
        return 0

    lax.fori_loop(0, TILES // 2, some_tiles, 0)


def first_block(step, spot, snp_index, table):
    vmem = pl.BlockSpec(memory_space=pltpu.VMEM)
    return pl.pallas_call(
        functools.partial(first_kernel, step),
        in_specs=[pl.BlockSpec(memory_space=pltpu.SMEM), vmem, vmem],
        out_shape=jax.ShapeDtypeStruct((K, BLOCK), jnp.float32),
        compiler_params=pltpu.CompilerParams(vmem_limit_bytes=8 * MIB),
        cost_estimate=estimate(3),
        name="first_block",
    )(spot, snp_index, table)


def geno_copy(step, block, geno_hbm, geno_ref, sem):
    span = pl.ds(pl.multiple_of(block * BLOCK, BLOCK), BLOCK)
    return pltpu.make_async_copy(geno_hbm.at[step, :, span], geno_ref, sem)


def block_sums(step, geno, freq, pt_ref, ps_ref, w_ref):
    n_ind, n_snp = geno.shape
    scale_j = scale_of_snp(iota((1, n_snp), 1))
    f1, f2, f3 = split3(freq * scale_j)
    b1, b2, _ = split3((1.0 - freq) * scale_j)
    h = jnp.dot(pt_ref[...], jnp.concatenate([f1, f2, f1, f3, f2, f1], 0), preferred_element_type=jnp.float32)
    w = jnp.concatenate([w_ref[...]] * (n_snp // LANES), 1)
    w = jnp.concatenate([w] * (n_ind // 64), 0)
    inv_a = pl.reciprocal(h, approx=True).astype(jnp.bfloat16)
    inv_b = pl.reciprocal(w - h, approx=True).astype(jnp.bfloat16)
    ratio_a = geno * inv_a
    ratio_b = (jnp.bfloat16(2) - geno) * inv_b
    ps = ps_ref[...]
    sum_a = jnp.dot(ps, ratio_a, preferred_element_type=jnp.float32)
    sum_b = jnp.dot(ps, ratio_b, preferred_element_type=jnp.float32)
    first = ratio_a - ratio_b if step == 0 else ratio_a
    num = lax.dot_general(jnp.concatenate([f1, f2], 0), first, NT, preferred_element_type=jnp.float32)
    if step:
        num += lax.dot_general(jnp.concatenate([b1, b2], 0), ratio_b, NT, preferred_element_type=jnp.float32)
    return sum_a[:K] + sum_a[K:], sum_b[:K] + sum_b[K:], num[:K] + num[K:]


def set_scales(w_ref):
    w_ref[...] = scale_of_ind(iota((64, LANES), 0)) * scale_of_snp(iota((64, LANES), 1))


def split_props(props, pt_ref, ps_ref):
    scaled = props * scale_of_ind(iota((1, props.shape[1]), 1))
    p1, p2, p3 = split3(scaled)
    ps_ref[...] = jnp.concatenate([p1, p2], 0)
    f = lambda v: v.astype(jnp.float32)
    stacked = jnp.concatenate([f(p1), f(p1), f(p2), f(p1), f(p2), f(p3)], 0)
    pt_ref[...] = stacked.T.astype(jnp.bfloat16)


def prepare_kernel(step, spot_ref, geno_hbm, props_ref, pt_ref, ps_ref, near_ref, own_ref, sems):
    spot = spot_ref[0]
    near = geno_copy(step, spot ^ 1, geno_hbm, near_ref, sems.at[0])
    own = geno_copy(step, spot, geno_hbm, own_ref, sems.at[1])
    near.start()
    own.start()
    split_props(props_ref[...], pt_ref, ps_ref)
    near.wait()
    own.wait()


def prepare(step, spot, genotypes, props):
    n_ind = genotypes.shape[1]
    smem, vmem = (pl.BlockSpec(memory_space=space) for space in (pltpu.SMEM, pltpu.VMEM))
    shape = lambda a, b: jax.ShapeDtypeStruct((a, b), jnp.bfloat16)
    return pl.pallas_call(
        functools.partial(prepare_kernel, step),
        in_specs=[smem, pl.BlockSpec(memory_space=pl.ANY), vmem],
        out_specs=[vmem] * 4,
        out_shape=[shape(n_ind, 6 * K), shape(2 * K, n_ind), shape(n_ind, BLOCK), shape(n_ind, BLOCK)],
        scratch_shapes=[pltpu.SemaphoreType.DMA((2,))],
        compiler_params=pltpu.CompilerParams(vmem_limit_bytes=47 * MIB),
        cost_estimate=estimate(2),
        name="prepare",
    )(spot, genotypes, props)


def far_kernel(step, spot_ref, geno_hbm, props_ref, index_ref, table_ref, *refs):
    if step:
        pt_ref, ps_ref, near_ref, first_ref, match_ref, *piece_refs = refs[:-9]
        *sums_refs, num_ref, own_ref, freq_ref, w_ref, geno_ref, sems = refs[-9:]
    else:
        *sums_refs, num_ref, own_ref, pt_ref, ps_ref, freq_ref, w_ref, geno_ref, sems = refs
    spot = spot_ref[0]
    fetch = lambda d: geno_copy(step, spot ^ d, geno_hbm, geno_ref.at[d - 1], sems.at[d - 1])

    def gather(d, half):
        for o in range(half * TILES // 2, (half + 1) * TILES // 2):
            if step and d == 1:
                here = slice(o * LANES, (o + 1) * LANES)
                found = (first_ref[0:8, here], first_ref[8:16, here])
                span = pl.ds(pl.multiple_of((spot ^ d) * BLOCK + o * LANES, LANES), LANES)
            else:
                found, span = gather_tile(step, spot ^ d, o, index_ref, table_ref)
            if step:
                found = overlay(found, span, spot, match_ref, piece_refs)
            put(freq_ref.at[d - 1] if d else own_ref, o, found)

    fetched = (2, 3) if step else (1, 2, 3)
    fetch(fetched[0]).start()
    set_scales(w_ref)
    if not step:
        split_props(props_ref[...], pt_ref, ps_ref)
    gather(1, 0)
    total = jnp.zeros(num_ref.shape, jnp.float32)
    order = [(d, half) for d in (1, 2, 3, 0) for half in (0, 1)]
    for (d, half), following in zip(order[:6], order[1:7]):
        if half == 0 and d in fetched:
            fetch(d).wait()
            if d < 3:
                fetch(d + 1).start()
        gather(*following)
        cols = slice(half * BLOCK // 2, (half + 1) * BLOCK // 2)
        geno = near_ref[:, cols] if step and d == 1 else geno_ref[d - 1, :, cols]
        sum_a, sum_b, num = block_sums(step, geno, freq_ref[d - 1, :, cols], pt_ref, ps_ref, w_ref)
        sums_refs[d - 1][0:K, cols] = sum_a
        sums_refs[d - 1][K:, cols] = sum_b
        total += num
    gather(0, 1)
    num_ref[...] = total


def far_sums(step, spot, genotypes, props, snp_index, table, extra):
    n_ind, n_snp = genotypes.shape[1:]
    assert n_snp == 4 * BLOCK
    smem, vmem = (pl.BlockSpec(memory_space=space) for space in (pltpu.SMEM, pltpu.VMEM))
    shape = lambda a, b, t=jnp.float32: jax.ShapeDtypeStruct((a, b), t)
    outs = [
        *[shape(2 * K, BLOCK)] * 3,
        shape(K, n_ind),
        shape(K, BLOCK),
    ]
    if step == 0:
        outs += [shape(n_ind, 6 * K, jnp.bfloat16), shape(2 * K, n_ind, jnp.bfloat16)]
    return pl.pallas_call(
        functools.partial(far_kernel, step),
        in_specs=[smem, pl.BlockSpec(memory_space=pl.ANY), *[vmem] * (3 + len(extra))],
        out_specs=[vmem] * len(outs),
        scratch_shapes=[
            pltpu.VMEM((3, K, BLOCK), jnp.float32),
            pltpu.VMEM((64, LANES), jnp.float32),
            pltpu.VMEM((3, n_ind, BLOCK), jnp.bfloat16),
            pltpu.SemaphoreType.DMA((3,)),
        ],
        out_shape=outs,
        compiler_params=pltpu.CompilerParams(vmem_limit_bytes=(40 if step else 62) * MIB),
        cost_estimate=estimate(14),
        name="far_sums",
    )(spot, genotypes, props, snp_index, table, *extra)


def own_kernel(step, spot_ref, geno_ref, freq_ref, pt_ref, ps_ref, before_ref, sums_ref, num_ref, w_ref):
    set_scales(w_ref)
    num_ref[...] = before_ref[...]

    def one_half(half, _):
        cols = pl.ds(pl.multiple_of(half * HALF, HALF), HALF)
        geno = geno_ref[:, cols] if step else geno_ref[0, :, cols]
        sum_a, sum_b, num = block_sums(step, geno, freq_ref[:, cols], pt_ref, ps_ref, w_ref)
        sums_ref[0:K, cols] = sum_a
        sums_ref[K:, cols] = sum_b
        num_ref[...] += num
        return 0

    lax.fori_loop(0, 2, one_half, 0)


def own_sums(step, spot, geno, freq, pt, ps, before):
    n_ind = pt.shape[0]
    outs = [jax.ShapeDtypeStruct((2 * K, BLOCK), jnp.float32), jax.ShapeDtypeStruct(before.shape, jnp.float32)]
    scratch = [pltpu.VMEM((64, LANES), jnp.float32)]
    if step:
        smem, vmem = (pl.BlockSpec(memory_space=space) for space in (pltpu.SMEM, pltpu.VMEM))
        layout = dict(in_specs=[smem] + [vmem] * 5, out_specs=[vmem] * 2, scratch_shapes=scratch)
    else:
        fixed = lambda j, s: (0, 0)
        layout = dict(
            grid_spec=pltpu.PrefetchScalarGridSpec(
                num_scalar_prefetch=1,
                grid=(1,),
                in_specs=[
                    pl.BlockSpec((1, n_ind, BLOCK), lambda j, s: (step, 0, s[0])),
                    *[pl.BlockSpec(a.shape, fixed) for a in (freq, pt, ps, before)],
                ],
                out_specs=[pl.BlockSpec(a.shape, fixed) for a in outs],
                scratch_shapes=scratch,
            )
        )
    return pl.pallas_call(
        functools.partial(own_kernel, step),
        out_shape=outs,
        compiler_params=pltpu.CompilerParams(vmem_limit_bytes=(40 if step else 62) * MIB),
        cost_estimate=estimate(5),
        name="own_sums",
        **layout,
    )(spot, geno, freq, pt, ps, before)


def finish_kernel(mine_ref, other_ref, old_ref, perm_ref, new_ref, hold_ref):
    sums = mine_ref[...] + other_ref[...]
    old = old_ref[...]
    acc_a = old * sums[:K]
    acc_b = (1.0 - old) * sums[K:]
    hold_ref[...] = acc_a / (acc_a + acc_b)
    for o in range(TILES):
        index = jnp.broadcast_to(perm_ref[o : o + 1, :], (8, LANES))
        zero = jnp.zeros((8, LANES), jnp.float32)
        top, bottom = pick_lanes(index, tiles_of(hold_ref, 0), (zero, zero))
        put(new_ref, o, (top, bottom))


def finish(mine, other, old, perm):
    return pl.pallas_call(
        finish_kernel,
        out_shape=jax.ShapeDtypeStruct(old.shape, jnp.float32),
        scratch_shapes=[pltpu.VMEM(old.shape, jnp.float32)],
        compiler_params=pltpu.CompilerParams(vmem_limit_bytes=4 * MIB),
        cost_estimate=estimate(1),
        name="finish",
    )(mine, other, old, perm)


def place_kernel(spot_ref, start_ref, pos_ref, table_ref, *refs):
    piece_refs, out_ref = refs[:-1], refs[-1]
    rows = pos_ref.shape[0]
    first = pl.program_id(0) * rows
    lane = iota((8, LANES), 1)
    def one_tile(o):
        span = pl.ds(pl.multiple_of(o * LANES, LANES), LANES)
        pos = jnp.broadcast_to(pos_ref[pl.ds(o, 1), :], (8, LANES))
        low, owner = pos & 127, pos >> 10
        top, bottom = table_ref[0:8, span], table_ref[8:16, span]
        for d, piece_ref in enumerate(piece_refs):
            piece = spot_ref[0] ^ d
            before = start_ref[piece, first + o]
            tile = jnp.minimum(before >> 7, TILES - 1)
            ends = [pl.ds(pl.multiple_of(t * LANES, LANES), LANES) for t in (tile, jnp.minimum(tile + 1, TILES - 1))]
            head = lane >= (before & 127)
            upper = jnp.where(head, piece_ref[0:8, ends[0]], piece_ref[0:8, ends[1]])
            lower = jnp.where(head, piece_ref[8:16, ends[0]], piece_ref[8:16, ends[1]])
            here = owner == piece
            top = jnp.where(here, jnp.take_along_axis(upper, low, axis=1), top)
            bottom = jnp.where(here, jnp.take_along_axis(lower, low, axis=1), bottom)
        out_ref[0:8, span], out_ref[8:16, span] = top, bottom

    def some_tiles(i, _):
        for o in range(16):
            one_tile(i * 16 + o)
        return 0

    lax.fori_loop(0, rows // 16, some_tiles, 0)


def place(table, pieces, pos, start, spot):
    rows = 32
    fixed = lambda i: (0, 0)
    return pl.pallas_call(
        place_kernel,
        grid=(pos.shape[0] // rows,),
        in_specs=[
            pl.BlockSpec(memory_space=pltpu.SMEM),
            pl.BlockSpec(memory_space=pltpu.SMEM),
            pl.BlockSpec((rows, LANES), lambda i: (i, 0)),
            pl.BlockSpec((K, rows * LANES), lambda i: (0, i)),
            *[pl.BlockSpec(p.shape, fixed) for p in pieces],
        ],
        out_specs=pl.BlockSpec((K, rows * LANES), lambda i: (0, i)),
        out_shape=jax.ShapeDtypeStruct(table.shape, jnp.float32),
        compiler_params=pltpu.CompilerParams(vmem_limit_bytes=16 * MIB),
        cost_estimate=estimate(4),
        name="place",
    )(spot, start, pos, table, *pieces)


def swap(value, axis, bits):
    size = lax.axis_size(axis)
    return lax.ppermute(value, axis, [(i, i ^ bits) for i in range(size)])


def all_sum4(value, axis, unit):
    one, two, three = (swap(value, axis, d * unit) for d in (1, 2, 3))
    return (value + one) + (two + three)


def together(*values):
    return lax.optimization_barrier(values)


def per_device(genotypes, snp_index, props, freq_table):
    batch_total = genotypes.shape[2] * lax.axis_size("snp")
    n_ind = genotypes.shape[1]
    spot = lax.axis_index("ind") // 8
    spot_array = jnp.reshape(spot, (1,)).astype(jnp.int32)
    extra = ()
    for step in range(STEPS):
        *far, num, old = far_sums(step, spot_array, genotypes, props, snp_index, freq_table, extra)
        if step == 0:
            *far, num, old, pt, ps = *far, num, old
            geno_own = genotypes
        parts = [swap(far[d - 1], "ind", 8 * d) for d in (1, 2, 3)]
        mine, num = own_sums(step, spot_array, geno_own, old, pt, ps, num)
        mine = (mine + parts[0]) + (parts[1] + parts[2])
        mine, held, indexes = together(mine, freq_table, snp_index)
        mine = all_sum4(mine, "ind", 2)
        across = swap(num, "snp", 1)
        pos, perm_a, start_a = index_part(step, (0, 1), indexes)
        num, across, pos = together(num, across, pos)
        num = num + across
        num, pos = together(num, pos)
        num = num + swap(num, "snp", 2)
        pos, perm_b, start_b, *match = index_part(step, (2, 3), indexes, (pos,))
        perm = jnp.concatenate([perm_a, perm_b])
        start = jnp.concatenate([start_a[:, 0], start_b[:, 0]])
        other = swap(mine, "ind", 1)
        mine, held, indexes = together(mine, freq_table, snp_index)
        if step == 0:
            beside = first_block(1, spot_array, indexes, held)
        else:
            beside = place(held, pieces, *maps, spot_array)
        other, beside = together(other, beside)
        maps = (pos, start)
        new = finish(mine, other, old, lax.dynamic_index_in_dim(perm, spot, 0, False))
        pieces = [new] + [swap(new, "ind", 8 * d) for d in (1, 2, 3)]
        prop_num = num * scale_of_ind(jnp.arange(n_ind))
        if step == 0:
            prop_num = 2.0 * batch_total + (prop_num - jnp.sum(props * prop_num, 0, keepdims=True))
        props = props * prop_num / (2.0 * batch_total)
        if step == 0:
            pt, ps, near, geno_own = prepare(1, spot_array, genotypes, together(props, new)[0])
            extra = (pt, ps, near, beside, *match, *pieces)
    return (jnp.log(props), place(beside, pieces, *maps, spot_array))


def solution(mesh):
    placed = (P(None, "ind", "snp"), P(None, "snp"), P(None, "ind"), P(None, "snp"))
    return jax.shard_map(
        per_device,
        mesh=mesh,
        in_specs=placed,
        out_specs=(P(None, "ind"), P(None, "snp")),
        check_vma=False,
    )
```

```python
import functools

import jax
import jax.numpy as jnp
import numpy as np
from jax import lax
from jax.experimental import pallas as pl
from jax.experimental.pallas import tpu as pltpu
from jax.sharding import PartitionSpec as P

STEPS = 2
K = 16
LANES = 128
BLOCK = 1024
TILES = BLOCK // LANES
HALF = BLOCK // 2
NN = (((1,), (0,)), ((), ()))
NT = (((1,), (1,)), ((), ()))
TN = (((0,), (0,)), ((), ()))
MIB = 1 << 20

def scale_of_ind(i):
    return ((i % 64 * 37 + 5) % 128 + 128).astype(jnp.float32) * (1.0 / 256)


def scale_of_snp(j):
    return ((j % 128 * 53 + 11) % 128 + 128).astype(jnp.float32) * (1.0 / 256)


def iota(shape, dim):
    return lax.broadcasted_iota(jnp.int32, shape, dim)


def estimate(us):
    return pl.CostEstimate(flops=0, bytes_accessed=int(us * 3.5e6), transcendentals=0)


def split3(x):
    one = x.astype(jnp.bfloat16)
    rest = x - one.astype(jnp.float32)
    two = rest.astype(jnp.bfloat16)
    three = (rest - two.astype(jnp.float32)).astype(jnp.bfloat16)
    return one, two, three


def dot_exact(left, right, dims):
    return lax.dot_general(
        left.astype(jnp.bfloat16), right.astype(jnp.bfloat16), dims, preferred_element_type=jnp.float32
    )


def one_hot(count, value):
    ids = lax.broadcasted_iota(jnp.int32, (count, value.shape[1]), 0)
    return (ids == value).astype(jnp.float32).astype(jnp.bfloat16)


def halves(x):
    hi = jnp.floor(x * (1.0 / LANES))
    return hi, x - LANES * hi


def look_up(table, hot_hi, hot_lo):
    hi, lo = halves(table)
    pick = hot_lo.astype(jnp.float32)
    first = jnp.sum(pick * dot_exact(hi, hot_hi, TN), 0, keepdims=True)
    return LANES * first + jnp.sum(pick * dot_exact(lo, hot_hi, TN), 0, keepdims=True)


def index_kernel(step, blocks, rows_ref, *refs):
    before_refs, (pos_ref, perm_ref, start_ref, *match_refs) = refs[: min(blocks[0], 1)], refs[min(blocks[0], 1) :]
    row = lax.broadcasted_iota(jnp.int32, (LANES, LANES), 0)
    col = lax.broadcasted_iota(jnp.int32, (LANES, LANES), 1)
    below = (col < row).astype(jnp.float32)
    above = (row < col).astype(jnp.float32)
    ones = jnp.ones((LANES, LANES), jnp.float32)
    local = lax.broadcasted_iota(jnp.int32, (1, BLOCK), 1).astype(jnp.float32)
    local_hi, local_lo = (v.astype(jnp.bfloat16) for v in halves(local))
    pos = before_refs[0][...].astype(jnp.float32) if before_refs else jnp.full((LANES, LANES), -1.0, jnp.float32)
    span_of = lambda b: pl.ds(pl.multiple_of(b * BLOCK, BLOCK), BLOCK)

    def one_block(b, pos):
        rows = rows_ref[step : step + 1, span_of(b)]
        hot_hi, hot_lo = one_hot(LANES, rows >> 7), one_hot(LANES, rows & 127)
        mask = dot_exact(hot_hi, hot_lo, NT)
        rank = dot_exact(dot_exact(below, mask, NN), ones, NN) + dot_exact(mask, above, NN)
        counts = dot_exact(jnp.ones((16, BLOCK), jnp.float32), hot_hi, NT)
        start_ref[b - blocks[0]] = dot_exact(counts, above, NN)[:8].astype(jnp.int32)
        rank_j = look_up(rank, hot_hi, hot_lo).astype(jnp.int32)
        hot_rank = one_hot(16, rank_j >> 7)
        hot_low = one_hot(LANES, rank_j & 127)
        perm = LANES * dot_exact(hot_rank * local_hi, hot_low, NT) + dot_exact(hot_rank * local_lo, hot_low, NT)
        perm_ref[b - blocks[0]] = perm[:TILES].astype(jnp.int32)
        return jnp.where(mask > 0.5, rank + (b * BLOCK).astype(jnp.float32), pos)

    pos = lax.fori_loop(blocks[0], blocks[-1] + 1, one_block, pos)
    pos_ref[...] = pos.astype(jnp.int32)
    for match_ref in match_refs:

        def one_match(b, _, match_ref=match_ref):
            rows = rows_ref[1:2, span_of(b)]
            found = look_up(pos + 1.0, one_hot(LANES, rows >> 7), one_hot(LANES, rows & 127))
            match_ref[0:1, span_of(b)] = found.astype(jnp.int32) - 1
            return 0

        lax.fori_loop(0, match_ref.shape[1] // BLOCK, one_match, 0)


def index_part(step, blocks, snp_index, before=()):
    n_snp = snp_index.shape[1]
    whole = lambda *shape: jax.ShapeDtypeStruct(shape, jnp.int32)
    last = blocks[-1] == n_snp // BLOCK - 1
    outs = [whole(LANES, LANES), whole(len(blocks), TILES, LANES), whole(len(blocks), 8, LANES)]
    return pl.pallas_call(
        functools.partial(index_kernel, step, blocks),
        out_shape=outs + ([whole(1, n_snp)] if last and step == 0 else []),
        compiler_params=pltpu.CompilerParams(vmem_limit_bytes=24 * MIB),
        cost_estimate=estimate(3),
        name="index_part",
    )(snp_index, *before)


def pick_lanes(index, sources, first):
    low, high = index & 127, index >> 7
    top, bottom = first
    for number, upper, lower in sources:
        here = high == number
        top = jnp.where(here, jnp.take_along_axis(upper, low, axis=1), top)
        bottom = jnp.where(here, jnp.take_along_axis(lower, low, axis=1), bottom)
    return top, bottom


def tiles_of(ref, base):
    for s in range(ref.shape[1] // LANES):
        span = slice(s * LANES, (s + 1) * LANES)
        yield base + s, ref[0:8, span], ref[8:16, span]


def put(ref, o, found):
    ref[0:8, o * LANES : (o + 1) * LANES] = found[0]
    ref[8:16, o * LANES : (o + 1) * LANES] = found[1]


def gather_tile(step, block, o, index_ref, table_ref):
    span = pl.ds(pl.multiple_of(block * BLOCK + o * LANES, LANES), LANES)
    zero = jnp.zeros((8, LANES), jnp.float32)
    index = jnp.broadcast_to(index_ref[step : step + 1, span], (8, LANES))
    return pick_lanes(index, tiles_of(table_ref, 0), (zero, zero)), span


def overlay(found, span, spot, match_ref, piece_refs):
    match = jnp.broadcast_to(match_ref[0:1, span], (8, LANES))
    for d, piece_ref in enumerate(piece_refs):
        found = pick_lanes(match, tiles_of(piece_ref, (spot ^ d) * TILES), found)
    return found


def first_kernel(step, spot_ref, index_ref, table_ref, out_ref):
    def some_tiles(i, _):
        for o in (2 * i, 2 * i + 1):
            found, _ = gather_tile(step, spot_ref[0] ^ 1, o, index_ref, table_ref)
            here = pl.ds(pl.multiple_of(o * LANES, LANES), LANES)
            out_ref[0:8, here], out_ref[8:16, here] = found
        return 0

    lax.fori_loop(0, TILES // 2, some_tiles, 0)


def first_block(step, spot, snp_index, table):
    vmem = pl.BlockSpec(memory_space=pltpu.VMEM)
    return pl.pallas_call(
        functools.partial(first_kernel, step),
        in_specs=[pl.BlockSpec(memory_space=pltpu.SMEM), vmem, vmem],
        out_shape=jax.ShapeDtypeStruct((K, BLOCK), jnp.float32),
        compiler_params=pltpu.CompilerParams(vmem_limit_bytes=8 * MIB),
        cost_estimate=estimate(3),
        name="first_block",
    )(spot, snp_index, table)


def geno_copy(step, block, geno_hbm, geno_ref, sem):
    span = pl.ds(pl.multiple_of(block * BLOCK, BLOCK), BLOCK)
    return pltpu.make_async_copy(geno_hbm.at[step, :, span], geno_ref, sem)


def block_sums(step, geno, freq, pt_ref, ps_ref, w_ref):
    n_ind, n_snp = geno.shape
    scale_j = scale_of_snp(iota((1, n_snp), 1))
    f1, f2, f3 = split3(freq * scale_j)
    b1, b2, _ = split3((1.0 - freq) * scale_j)
    h = jnp.dot(pt_ref[...], jnp.concatenate([f1, f2, f1, f3, f2, f1], 0), preferred_element_type=jnp.float32)
    w = jnp.concatenate([w_ref[...]] * (n_snp // LANES), 1)
    w = jnp.concatenate([w] * (n_ind // 64), 0)
    inv_a = pl.reciprocal(h, approx=True).astype(jnp.bfloat16)
    inv_b = pl.reciprocal(w - h, approx=True).astype(jnp.bfloat16)
    ratio_a = geno * inv_a
    ratio_b = (jnp.bfloat16(2) - geno) * inv_b
    ps = ps_ref[...]
    sum_a = jnp.dot(ps, ratio_a, preferred_element_type=jnp.float32)
    sum_b = jnp.dot(ps, ratio_b, preferred_element_type=jnp.float32)
    first = ratio_a - ratio_b if step == 0 else ratio_a
    num = lax.dot_general(jnp.concatenate([f1, f2], 0), first, NT, preferred_element_type=jnp.float32)
    if step:
        num += lax.dot_general(jnp.concatenate([b1, b2], 0), ratio_b, NT, preferred_element_type=jnp.float32)
    return sum_a[:K] + sum_a[K:], sum_b[:K] + sum_b[K:], num[:K] + num[K:]


def set_scales(w_ref):
    w_ref[...] = scale_of_ind(iota((64, LANES), 0)) * scale_of_snp(iota((64, LANES), 1))


def split_props(props, pt_ref, ps_ref):
    scaled = props * scale_of_ind(iota((1, props.shape[1]), 1))
    p1, p2, p3 = split3(scaled)
    ps_ref[...] = jnp.concatenate([p1, p2], 0)
    f = lambda v: v.astype(jnp.float32)
    stacked = jnp.concatenate([f(p1), f(p1), f(p2), f(p1), f(p2), f(p3)], 0)
    pt_ref[...] = stacked.T.astype(jnp.bfloat16)


def prepare_kernel(step, spot_ref, geno_hbm, props_ref, pt_ref, ps_ref, near_ref, own_ref, sems):
    spot = spot_ref[0]
    near = geno_copy(step, spot ^ 1, geno_hbm, near_ref, sems.at[0])
    own = geno_copy(step, spot, geno_hbm, own_ref, sems.at[1])
    near.start()
    own.start()
    split_props(props_ref[...], pt_ref, ps_ref)
    near.wait()
    own.wait()


def prepare(step, spot, genotypes, props):
    n_ind = genotypes.shape[1]
    smem, vmem = (pl.BlockSpec(memory_space=space) for space in (pltpu.SMEM, pltpu.VMEM))
    shape = lambda a, b: jax.ShapeDtypeStruct((a, b), jnp.bfloat16)
    return pl.pallas_call(
        functools.partial(prepare_kernel, step),
        in_specs=[smem, pl.BlockSpec(memory_space=pl.ANY), vmem],
        out_specs=[vmem] * 4,
        out_shape=[shape(n_ind, 6 * K), shape(2 * K, n_ind), shape(n_ind, BLOCK), shape(n_ind, BLOCK)],
        scratch_shapes=[pltpu.SemaphoreType.DMA((2,))],
        compiler_params=pltpu.CompilerParams(vmem_limit_bytes=47 * MIB),
        cost_estimate=estimate(2),
        name="prepare",
    )(spot, genotypes, props)


def far_kernel(step, spot_ref, geno_hbm, props_ref, index_ref, table_ref, *refs):
    if step:
        pt_ref, ps_ref, near_ref, first_ref, match_ref, *piece_refs = refs[:-9]
        *sums_refs, num_ref, own_ref, freq_ref, w_ref, geno_ref, sems = refs[-9:]
    else:
        *sums_refs, num_ref, own_ref, pt_ref, ps_ref, freq_ref, w_ref, geno_ref, sems = refs
    spot = spot_ref[0]
    fetch = lambda d: geno_copy(step, spot ^ d, geno_hbm, geno_ref.at[d - 1], sems.at[d - 1])

    def gather(d, half):
        for o in range(half * TILES // 2, (half + 1) * TILES // 2):
            if step and d == 1:
                here = slice(o * LANES, (o + 1) * LANES)
                found = (first_ref[0:8, here], first_ref[8:16, here])
                span = pl.ds(pl.multiple_of((spot ^ d) * BLOCK + o * LANES, LANES), LANES)
            else:
                found, span = gather_tile(step, spot ^ d, o, index_ref, table_ref)
            if step:
                found = overlay(found, span, spot, match_ref, piece_refs)
            put(freq_ref.at[d - 1] if d else own_ref, o, found)

    fetched = (2, 3) if step else (1, 2, 3)
    fetch(fetched[0]).start()
    set_scales(w_ref)
    if not step:
        split_props(props_ref[...], pt_ref, ps_ref)
    gather(1, 0)
    total = jnp.zeros(num_ref.shape, jnp.float32)
    order = [(d, half) for d in (1, 2, 3, 0) for half in (0, 1)]
    for (d, half), following in zip(order[:6], order[1:7]):
        if half == 0 and d in fetched:
            fetch(d).wait()
            if d < 3:
                fetch(d + 1).start()
        gather(*following)
        cols = slice(half * BLOCK // 2, (half + 1) * BLOCK // 2)
        geno = near_ref[:, cols] if step and d == 1 else geno_ref[d - 1, :, cols]
        sum_a, sum_b, num = block_sums(step, geno, freq_ref[d - 1, :, cols], pt_ref, ps_ref, w_ref)
        sums_refs[d - 1][0:K, cols] = sum_a
        sums_refs[d - 1][K:, cols] = sum_b
        total += num
    gather(0, 1)
    num_ref[...] = total


def far_sums(step, spot, genotypes, props, snp_index, table, extra):
    n_ind, n_snp = genotypes.shape[1:]
    assert n_snp == 4 * BLOCK
    smem, vmem = (pl.BlockSpec(memory_space=space) for space in (pltpu.SMEM, pltpu.VMEM))
    shape = lambda a, b, t=jnp.float32: jax.ShapeDtypeStruct((a, b), t)
    outs = [
        *[shape(2 * K, BLOCK)] * 3,
        shape(K, n_ind),
        shape(K, BLOCK),
    ]
    if step == 0:
        outs += [shape(n_ind, 6 * K, jnp.bfloat16), shape(2 * K, n_ind, jnp.bfloat16)]
    return pl.pallas_call(
        functools.partial(far_kernel, step),
        in_specs=[smem, pl.BlockSpec(memory_space=pl.ANY), *[vmem] * (3 + len(extra))],
        out_specs=[vmem] * len(outs),
        scratch_shapes=[
            pltpu.VMEM((3, K, BLOCK), jnp.float32),
            pltpu.VMEM((64, LANES), jnp.float32),
            pltpu.VMEM((3, n_ind, BLOCK), jnp.bfloat16),
            pltpu.SemaphoreType.DMA((3,)),
        ],
        out_shape=outs,
        compiler_params=pltpu.CompilerParams(vmem_limit_bytes=(40 if step else 62) * MIB),
        cost_estimate=estimate(14),
        name="far_sums",
    )(spot, genotypes, props, snp_index, table, *extra)


def own_kernel(step, spot_ref, geno_ref, freq_ref, pt_ref, ps_ref, before_ref, sums_ref, num_ref, w_ref):
    set_scales(w_ref)
    num_ref[...] = before_ref[...]

    def one_half(half, _):
        cols = pl.ds(pl.multiple_of(half * HALF, HALF), HALF)
        geno = geno_ref[:, cols] if step else geno_ref[0, :, cols]
        sum_a, sum_b, num = block_sums(step, geno, freq_ref[:, cols], pt_ref, ps_ref, w_ref)
        sums_ref[0:K, cols] = sum_a
        sums_ref[K:, cols] = sum_b
        num_ref[...] += num
        return 0

    lax.fori_loop(0, 2, one_half, 0)


def own_sums(step, spot, geno, freq, pt, ps, before):
    n_ind = pt.shape[0]
    outs = [jax.ShapeDtypeStruct((2 * K, BLOCK), jnp.float32), jax.ShapeDtypeStruct(before.shape, jnp.float32)]
    scratch = [pltpu.VMEM((64, LANES), jnp.float32)]
    if step:
        smem, vmem = (pl.BlockSpec(memory_space=space) for space in (pltpu.SMEM, pltpu.VMEM))
        layout = dict(in_specs=[smem] + [vmem] * 5, out_specs=[vmem] * 2, scratch_shapes=scratch)
    else:
        fixed = lambda j, s: (0, 0)
        layout = dict(
            grid_spec=pltpu.PrefetchScalarGridSpec(
                num_scalar_prefetch=1,
                grid=(1,),
                in_specs=[
                    pl.BlockSpec((1, n_ind, BLOCK), lambda j, s: (step, 0, s[0])),
                    *[pl.BlockSpec(a.shape, fixed) for a in (freq, pt, ps, before)],
                ],
                out_specs=[pl.BlockSpec(a.shape, fixed) for a in outs],
                scratch_shapes=scratch,
            )
        )
    return pl.pallas_call(
        functools.partial(own_kernel, step),
        out_shape=outs,
        compiler_params=pltpu.CompilerParams(vmem_limit_bytes=(40 if step else 62) * MIB),
        cost_estimate=estimate(5),
        name="own_sums",
        **layout,
    )(spot, geno, freq, pt, ps, before)


def finish_kernel(mine_ref, other_ref, old_ref, perm_ref, new_ref, hold_ref):
    sums = mine_ref[...] + other_ref[...]
    old = old_ref[...]
    acc_a = old * sums[:K]
    acc_b = (1.0 - old) * sums[K:]
    hold_ref[...] = acc_a / (acc_a + acc_b)
    for o in range(TILES):
        index = jnp.broadcast_to(perm_ref[o : o + 1, :], (8, LANES))
        zero = jnp.zeros((8, LANES), jnp.float32)
        top, bottom = pick_lanes(index, tiles_of(hold_ref, 0), (zero, zero))
        put(new_ref, o, (top, bottom))


def finish(mine, other, old, perm):
    return pl.pallas_call(
        finish_kernel,
        out_shape=jax.ShapeDtypeStruct(old.shape, jnp.float32),
        scratch_shapes=[pltpu.VMEM(old.shape, jnp.float32)],
        compiler_params=pltpu.CompilerParams(vmem_limit_bytes=4 * MIB),
        cost_estimate=estimate(1),
        name="finish",
    )(mine, other, old, perm)


def place_kernel(spot_ref, start_ref, pos_ref, table_ref, *refs):
    piece_refs, out_ref = refs[:-1], refs[-1]
    rows = pos_ref.shape[0]
    first = pl.program_id(0) * rows
    lane = iota((8, LANES), 1)
    def one_tile(o):
        span = pl.ds(pl.multiple_of(o * LANES, LANES), LANES)
        pos = jnp.broadcast_to(pos_ref[pl.ds(o, 1), :], (8, LANES))
        low, owner = pos & 127, pos >> 10
        top, bottom = table_ref[0:8, span], table_ref[8:16, span]
        for d, piece_ref in enumerate(piece_refs):
            piece = spot_ref[0] ^ d
            before = start_ref[piece, first + o]
            tile = jnp.minimum(before >> 7, TILES - 1)
            ends = [pl.ds(pl.multiple_of(t * LANES, LANES), LANES) for t in (tile, jnp.minimum(tile + 1, TILES - 1))]
            head = lane >= (before & 127)
            upper = jnp.where(head, piece_ref[0:8, ends[0]], piece_ref[0:8, ends[1]])
            lower = jnp.where(head, piece_ref[8:16, ends[0]], piece_ref[8:16, ends[1]])
            here = owner == piece
            top = jnp.where(here, jnp.take_along_axis(upper, low, axis=1), top)
            bottom = jnp.where(here, jnp.take_along_axis(lower, low, axis=1), bottom)
        out_ref[0:8, span], out_ref[8:16, span] = top, bottom

    def some_tiles(i, _):
        for o in range(16):
            one_tile(i * 16 + o)
        return 0

    lax.fori_loop(0, rows // 16, some_tiles, 0)


def place(table, pieces, pos, start, spot):
    rows = 32
    fixed = lambda i: (0, 0)
    return pl.pallas_call(
        place_kernel,
        grid=(pos.shape[0] // rows,),
        in_specs=[
            pl.BlockSpec(memory_space=pltpu.SMEM),
            pl.BlockSpec(memory_space=pltpu.SMEM),
            pl.BlockSpec((rows, LANES), lambda i: (i, 0)),
            pl.BlockSpec((K, rows * LANES), lambda i: (0, i)),
            *[pl.BlockSpec(p.shape, fixed) for p in pieces],
        ],
        out_specs=pl.BlockSpec((K, rows * LANES), lambda i: (0, i)),
        out_shape=jax.ShapeDtypeStruct(table.shape, jnp.float32),
        compiler_params=pltpu.CompilerParams(vmem_limit_bytes=16 * MIB),
        cost_estimate=estimate(4),
        name="place",
    )(spot, start, pos, table, *pieces)


def swap(value, axis, bits):
    size = lax.axis_size(axis)
    return lax.ppermute(value, axis, [(i, i ^ bits) for i in range(size)])


def all_sum4(value, axis, unit):
    one, two, three = (swap(value, axis, d * unit) for d in (1, 2, 3))
    return (value + one) + (two + three)


def together(*values):
    return lax.optimization_barrier(values)


def per_device(genotypes, snp_index, props, freq_table):
    batch_total = genotypes.shape[2] * lax.axis_size("snp")
    n_ind = genotypes.shape[1]
    spot = lax.axis_index("ind") // 8
    spot_array = jnp.reshape(spot, (1,)).astype(jnp.int32)
    extra = ()
    for step in range(STEPS):
        *far, num, old = far_sums(step, spot_array, genotypes, props, snp_index, freq_table, extra)
        if step == 0:
            *far, num, old, pt, ps = *far, num, old
            geno_own = genotypes
        parts = [swap(far[d - 1], "ind", 8 * d) for d in (1, 2, 3)]
        mine, num = own_sums(step, spot_array, geno_own, old, pt, ps, num)
        mine = (mine + parts[0]) + (parts[1] + parts[2])
        mine, held, indexes = together(mine, freq_table, snp_index)
        mine = all_sum4(mine, "ind", 2)
        across = swap(num, "snp", 1)
        pos, perm_a, start_a = index_part(step, (0, 1), indexes)
        num, across, pos = together(num, across, pos)
        num = num + across
        num, pos = together(num, pos)
        if step == 1:
            across = swap(num, "snp", 2)
        pos, perm_b, start_b, *match = index_part(step, (2, 3), indexes, (pos,))
        perm = jnp.concatenate([perm_a, perm_b])
        start = jnp.concatenate([start_a[:, 0], start_b[:, 0]])
        mine, perm = together(mine, perm)
        other = swap(mine, "ind", 1)
        mine, held, indexes = together(mine, freq_table, snp_index)
        if step == 0:
            beside = first_block(1, spot_array, indexes, held)
            num, beside = together(num, beside)
            across = swap(num, "snp", 2)
        else:
            beside = place(held, pieces, *maps, spot_array)
        other, beside = together(other, beside)
        maps = (pos, start)
        new = finish(mine, other, old, lax.dynamic_index_in_dim(perm, spot, 0, False))
        pieces = [new] + [swap(new, "ind", 8 * d) for d in (1, 2, 3)]
        across, num, _ = together(across, num, new)
        prop_num = (num + across) * scale_of_ind(jnp.arange(n_ind))
        if step == 0:
            prop_num = 2.0 * batch_total + (prop_num - jnp.sum(props * prop_num, 0, keepdims=True))
        props = props * prop_num / (2.0 * batch_total)
        if step == 0:
            pt, ps, near, geno_own = prepare(1, spot_array, genotypes, together(props, new)[0])
            extra = (pt, ps, near, beside, *match, *pieces)
    return (jnp.log(props), place(beside, pieces, *maps, spot_array))


def solution(mesh):
    placed = (P(None, "ind", "snp"), P(None, "snp"), P(None, "ind"), P(None, "snp"))
    return jax.shard_map(
        per_device,
        mesh=mesh,
        in_specs=placed,
        out_specs=(P(None, "ind"), P(None, "snp")),
        check_vma=False,
    )
```
